128 devices in a mesh: cells: 16 (over y_lo, x, core), spots: 8 (over y_hi, z).
Axes of the slice: x: 4, y: 4 (y_hi: 2, y_lo: 2; y = y_hi * 2 + y_lo), z: 4, core: 2. Of those that a mesh axis runs over, the one named last changes fastest.
Arguments:
- cell_feat: bfloat16 [16384, 64], P('cells')
- spot_feat: bfloat16 [32768, 64], P('spots')
- cell_mass: float32 [16384], P('cells'), may hold values from 0.02 to 5
- spot_mass: float32 [32768], P('spots'), may hold values from 0.02 to 5
- block_pattern: int32 [128, 256], P('cells', 'spots'), may hold values from 0 to 1, as said below
Outputs:
- cell_pot: float32 [16384], P('cells')
- spot_pot: float32 [32768], P('spots')
- cell_map: float32 [16384, 64], P('cells')
- spot_map: float32 [32768, 64], P('spots')
The draws below stay inside these ranges and needn't reach their ends.
Inputs may be any that keep to these rules, and one draw needn't show every extreme that they name: `block_pattern`: every cluster block row and every cluster block column holds at least one allowed pair; the share of allowed blocks differs between cell cluster rows.
All inputs are finite; a program needn't handle non-finite values.
Results may differ from the reference program's by a relative error of at most 0.0024.
Values sent between devices are 32-bit elements; how exact they have to be, the bound alone decides.
A program may use at most 64 MiB of HBM per device.

```python
import math
import jax
import jax.numpy as jnp
from jax import lax

FEAT = 64
CLUSTER = 128
ITERS = 5
CELLS_ALL = 16384
SPOTS_ALL = 32768


def profile_draw(key, count):
    values = jax.random.normal(jax.random.fold_in(key, 13), (count, FEAT), jnp.float32)
    return values.astype(jnp.bfloat16)


def draw_cell_feat(key, part):
    key = jax.random.fold_in(key, 1)
    return profile_draw(key, CELLS_ALL)


def draw_spot_feat(key, part):
    key = jax.random.fold_in(key, 2)
    return profile_draw(key, SPOTS_ALL)


def draw_block_pattern(key, part):
    key = jax.random.fold_in(key, 3)
    row_blocks = CELLS_ALL // CLUSTER
    col_blocks = SPOTS_ALL // CLUSTER
    level = jax.random.randint(jax.random.fold_in(key, 21), (row_blocks, 1), 1, 9)
    noise = jax.random.randint(jax.random.fold_in(key, 22), (row_blocks, col_blocks), 0, 64)
    rows = jnp.arange(row_blocks, dtype=jnp.int32)[:, None]
    cols = jnp.arange(col_blocks, dtype=jnp.int32)[None, :]
    band_rows = cols == rows * col_blocks // row_blocks
    band_cols = rows == cols * row_blocks // col_blocks
    chosen = (noise < level) | band_rows | band_cols
    return jnp.where(chosen, 1, 0).astype(jnp.int32)


def block_levels(stream_key, extent, split, smallest, largest):
    def one(position, parts):
        draws = jax.random.uniform(jax.random.fold_in(jax.random.fold_in(stream_key, 6), position), (parts,), jnp.float32, smallest / len(split), largest / len(split))
        return jnp.repeat(jnp.exp(draws), extent[position] // parts).reshape((-1,) + (1,) * (len(extent) - position - 1))

    factor_of = one(*split[0])
    for cut in split[1:]:
        factor_of = factor_of * one(*cut)
    return factor_of


def setup_inputs(seed: int = 0) -> dict:
    splits = jax.random.split(jax.random.key(seed), 6)
    cell_feat = draw_cell_feat(jax.random.fold_in(splits[5], 71), 0)
    spot_feat = draw_spot_feat(jax.random.fold_in(splits[5], 71), 0)
    cell_mass = jnp.clip(jnp.exp(math.log(5.0) - 5.521461 * jax.random.uniform(splits[2], (CELLS_ALL,), jnp.float32) ** block_levels(splits[2], (CELLS_ALL,), ((0, 16),), -0.2, 0.2)), 0.02, 5.0)
    spot_mass = jnp.clip(jnp.exp(math.log(5.0) - 5.521461 * jax.random.uniform(splits[3], (SPOTS_ALL,), jnp.float32) ** block_levels(splits[3], (SPOTS_ALL,), ((0, 8),), -0.2, 0.2)), 0.02, 5.0)
    block_pattern = draw_block_pattern(jax.random.fold_in(splits[5], 71), 0)
    return {"cell_feat": cell_feat, "spot_feat": spot_feat, "cell_mass": cell_mass, "spot_mass": spot_mass, "block_pattern": block_pattern}


EPSILON = 0.05
NEG = -1e30


def allowed_tile(pattern):
    count_a, count_b = pattern.shape
    full = jnp.broadcast_to(pattern[:, None, :, None] > 0, (count_a, CLUSTER, count_b, CLUSTER))
    return full.reshape(count_a * CLUSTER, count_b * CLUSTER)


def half_step(own_feat, other_feat, other_pot, own_mass, pattern):
    total_own = own_feat.shape[0]
    span = min(512, total_own)
    blocks = total_own // span
    own_norm = jnp.sum(own_feat.astype(jnp.float32) ** 2, axis=1)
    other_norm = jnp.sum(other_feat.astype(jnp.float32) ** 2, axis=1)
    feat_blocks = own_feat.reshape(blocks, span, own_feat.shape[1])
    norm_blocks = own_norm.reshape(blocks, span)
    mass_blocks = own_mass.reshape(blocks, span)
    pattern_blocks = pattern.reshape(blocks, span // CLUSTER, pattern.shape[1])

    def one_block(items):
        feat_b, norm_b, mass_b, pattern_b = items
        cross = jnp.dot(feat_b, other_feat.T, preferred_element_type=jnp.float32)
        cost = (norm_b[:, None] + other_norm[None, :] - 2.0 * cross) / FEAT
        score = (other_pot[None, :] - cost) / EPSILON
        allow = allowed_tile(pattern_b)
        peak = jnp.max(jnp.where(allow, score, NEG), axis=1)
        weights = jnp.where(allow, jnp.exp(score - peak[:, None]), 0.0)
        total = jnp.sum(weights, axis=1)
        potential = EPSILON * (jnp.log(mass_b) - peak - jnp.log(total))
        mapped = jnp.dot(weights.astype(jnp.bfloat16), other_feat, preferred_element_type=jnp.float32) / total[:, None]
        return potential, mapped

    potential, mapped = lax.map(one_block, (feat_blocks, norm_blocks, mass_blocks, pattern_blocks))
    return potential.reshape(total_own), mapped.reshape(total_own, own_feat.shape[1])


def reference(cell_feat, spot_feat, cell_mass, spot_mass, block_pattern):
    spot_pot = jnp.zeros((spot_feat.shape[0],), jnp.float32)
    for step in range(ITERS):
        cell_pot, cell_map = half_step(cell_feat, spot_feat, spot_pot, cell_mass, block_pattern)
        spot_pot, spot_map = half_step(spot_feat, cell_feat, cell_pot, spot_mass, block_pattern.T)
    return cell_pot, spot_pot, cell_map, spot_map
```

```python
import functools
import math

import jax
import jax.numpy as jnp
from jax import lax
from jax.experimental import pallas as pl
from jax.experimental.pallas import tpu as pltpu
from jax.sharding import PartitionSpec as P

FEAT = 64
BLK = 128
ITERS = 5
EPSILON = 0.05
NEG = -1e30
LOG2E = math.log2(math.e)
UNIT = LOG2E / EPSILON
CROSS = UNIT * 2.0 / FEAT
NORM = UNIT / FEAT
SIDE = 16
MSG = FEAT + 8
MESH = pl.DeviceIdType.MESH
F32 = jnp.float32
BF16 = jnp.bfloat16


def log2(v):
    return jnp.log(v) * LOG2E


def wait_for(view, sem):
    pltpu.make_async_copy(view, view, sem).wait()


def send(src, dst, ssem, rsem, dev):
    pltpu.make_async_remote_copy(
        src_ref=src, dst_ref=dst, send_sem=ssem, recv_sem=rsem, device_id=dev, device_id_type=MESH
    ).start()


def within(index, top):
    return jnp.minimum(jnp.maximum(index, 0), top)


def ring(offset):
    return {0: 0, 1: 1, 2: 2, 3: 1}[offset]


def lane_spread(pot, out):
    full = jnp.concatenate([pot, jnp.zeros((BLK - SIDE, BLK), F32)], axis=0)
    turned = jnp.transpose(full)
    for b in range(SIDE):
        out[b] = jnp.broadcast_to(turned[:, b : b + 1], (BLK, BLK))


def sinkhorn_kernel(
    cap, cfeat, sfeat, cmass, smass, pattern,
    cpot_out, spot_out, cmap_out, smap_out, flag_out,
    swap_out, swap_in, side_out, side_in, chh, cht, shh, sht, cross, crosst, spread,
    blockmap, slot_peak, peak_scr, list_v, list_s, tab_v, tab_s,
    buf_e, buf_d, flag_e, flag_d, msg_c, rcv_c, msg_s, rcv_s, own_c, own_s, pot_s,
    sem_swap, sem_e, sem_d, sem_map, sem_loc,
):
    ci = lax.axis_index("cells")
    si = lax.axis_index("spots")
    core = ci % 2
    dme = ci // 2
    ylo, xx = dme // 4, dme % 4
    yhi, zz = si // 4, si % 4
    eme = si * 2 + core
    partner = (ci + 1 - 2 * core, si)

    e_peers = []
    for a in range(2):
        for b in range(4):
            for k in range(2):
                if a or b or k:
                    s2 = lax.rem(yhi + a, 2) * 4 + lax.rem(zz + b, 4)
                    k2 = lax.rem(core + k, 2)
                    e_peers.append((2 * a + ring(b) + 0.1 * k, (dme * 2 + k2, s2), s2, k2))
    e_peers.sort(key=lambda item: -item[0])
    d_peers = []
    for a in range(2):
        for b in range(4):
            if a or b:
                d2 = lax.rem(ylo + a, 2) * 4 + lax.rem(xx + b, 4)
                d_peers.append((a + ring(b), (d2 * 2 + core, si), d2))
    d_peers.sort(key=lambda item: -item[0])

    barrier = pltpu.get_barrier_semaphore()
    for item in e_peers + d_peers:
        pl.semaphore_signal(barrier, inc=1, device_id=item[1], device_id_type=MESH)

    def own_cells(b, _):
        block = cfeat[:, pl.ds(pl.multiple_of(b * BLK, BLK), BLK)]
        wide = block.astype(F32)
        swap_out[b] = wide
        chh[core * 8 + b] = block
        cht[core * 8 + b] = jnp.transpose(wide).astype(BF16)
        return 0

    lax.fori_loop(0, 8, own_cells, 0)

    def own_spots(b, norms):
        block = sfeat[:, pl.ds(pl.multiple_of((core * SIDE + b) * BLK, BLK), BLK)]
        wide = block.astype(F32)
        shh[b] = block
        sht[b] = jnp.transpose(wide).astype(BF16)
        here = lax.broadcasted_iota(jnp.int32, (SIDE, BLK), 0) == b
        return jnp.where(here, jnp.sum(wide * wide, axis=0, keepdims=True) * NORM, norms)

    spot_norm = lax.fori_loop(0, SIDE, own_spots, jnp.zeros((SIDE, BLK), F32))
    pattern_own = (pattern[...] > 0).astype(F32)
    side_out[0] = cmass[...]
    side_out[1] = jnp.concatenate([pattern_own, jnp.zeros((8, BLK - 32), F32)], axis=1)

    pl.semaphore_wait(barrier, len(e_peers) + len(d_peers))

    send(side_out, side_in, sem_swap.at[0], sem_swap.at[1], partner)
    send(swap_out, swap_in, sem_swap.at[2], sem_swap.at[3], partner)
    wait_for(side_in, sem_swap.at[1])

    first = core == 0
    mine, theirs = side_out[1], side_in[1]
    lane = lax.broadcasted_iota(jnp.int32, (SIDE, BLK), 1)
    both = jnp.concatenate(
        [jnp.where(first, mine, theirs), jnp.where(first, theirs, mine)], axis=0
    )
    both = jnp.where((lane >= core * SIDE) & (lane < core * SIDE + SIDE), both, 0.0)
    upto = (
        lax.broadcasted_iota(jnp.int32, (BLK, BLK), 0)
        < lax.broadcasted_iota(jnp.int32, (BLK, BLK), 1)
    ).astype(BF16)
    inside = jnp.dot(both.astype(BF16), upto, preferred_element_type=F32)
    per_row = jnp.broadcast_to(jnp.sum(both, axis=1, keepdims=True), (SIDE, BLK))
    earlier = (
        lax.broadcasted_iota(jnp.int32, (SIDE, SIDE), 1)
        < lax.broadcasted_iota(jnp.int32, (SIDE, SIDE), 0)
    ).astype(BF16)
    before = jnp.dot(earlier, per_row.astype(BF16), preferred_element_type=F32)
    place = jnp.where(both > 0, before + inside, -1.0)
    count = jnp.sum(jnp.sum(both, axis=1, keepdims=True), axis=0, keepdims=True)
    over = jnp.broadcast_to(jnp.where(count > cap, 1.0, 0.0), (8, BLK))
    width = list_v.shape[1]
    pairs = SIDE * SIDE
    wide_place = jnp.broadcast_to(place[:, None, :], (SIDE, SIDE, BLK)).reshape(pairs, BLK)
    pair = lax.broadcasted_iota(jnp.int32, (pairs, BLK), 0)
    pair_lane = lax.broadcasted_iota(jnp.int32, (pairs, BLK), 1)
    chosen = pair_lane == core * SIDE + pair % SIDE
    slot_of = jnp.sum(jnp.where(chosen, wide_place, 0.0), axis=1, keepdims=True)
    hot = slot_of == lax.broadcasted_iota(jnp.int32, (pairs, width), 1).astype(F32)
    kind = lax.broadcasted_iota(jnp.int32, (8, pairs), 0)
    which = lax.broadcasted_iota(jnp.int32, (8, pairs), 1)
    facts = jnp.where(kind == 0, which // SIDE, jnp.where(kind == 1, which % SIDE, 1))
    lists = jnp.dot(
        facts.astype(F32).astype(BF16), hot.astype(F32).astype(BF16), preferred_element_type=F32
    )
    none = 99.0 * (1.0 - lists[2:3])
    kind = lax.broadcasted_iota(jnp.int32, (8, width), 0)
    lists = jnp.where(kind >= 2, 0.0, lists) + jnp.where(
        kind == 2, lists[0:1] + none, jnp.where(kind == 3, lists[1:2] + none, 0.0)
    )
    list_v[...] = lists.astype(jnp.int32)
    tab_v[...] = jnp.where((place < 0) | (place >= cap), float(cap), place).astype(jnp.int32)
    copies = [
        pltpu.make_async_copy(list_v, list_s, sem_loc.at[0]),
        pltpu.make_async_copy(tab_v, tab_s, sem_loc.at[1]),
    ]
    for copy in copies:
        copy.start()
    flag_e[eme] = over
    for _, dev, _, _ in e_peers:
        send(flag_e.at[eme], flag_e.at[eme], sem_e.at[0, ITERS], sem_e.at[1, ITERS], dev)

    cell_log = log2(
        jnp.concatenate(
            [
                jnp.where(first, side_out[0], side_in[0]),
                jnp.where(first, side_in[0], side_out[0]),
            ],
            axis=0,
        )
    )
    spot_log = log2(smass[pl.ds(pl.multiple_of(core * SIDE, SIDE), SIDE), :])

    lane_spread(-spot_norm, spread)
    wait_for(swap_in, sem_swap.at[3])

    def other_cells(b, _):
        wide = swap_in[b]
        chh[(1 - core) * 8 + b] = wide.astype(BF16)
        cht[(1 - core) * 8 + b] = jnp.transpose(wide).astype(BF16)
        return 0

    lax.fori_loop(0, 8, other_cells, 0)
    for copy in copies:
        copy.wait()

    step = 4

    def build(i, _):
        for k in range(step):
            e = i * step + k
            r = within(list_s[0, e], SIDE - 1)
            c = within(list_s[1, e], SIDE - 1)
            cross[e] = jnp.dot(cht[r], shh[c], preferred_element_type=F32) * CROSS
            crosst[e] = jnp.dot(sht[c], chh[r], preferred_element_type=F32) * CROSS
        return 0

    lax.fori_loop(0, cap // step, build, 0)

    rows = lax.broadcasted_iota(jnp.int32, (SIDE, BLK), 0)

    def half(scores, other, own, feats):
        def body(i, carry):
            peak, total = carry
            parts = []
            for k in range(step):
                e = i * step + k
                o = within(list_s[other, e], SIDE - 1)
                v = scores[e] + spread[o]
                top = jnp.max(v, axis=0, keepdims=True)
                p = jnp.exp2(v - top)
                parts.append((list_s[own + 2, e], top, jnp.sum(p, axis=0, keepdims=True)))
                if feats is not None:
                    slot_peak[e] = top
                    blockmap[e] = jnp.dot(
                        feats[o], p.astype(BF16), preferred_element_type=F32
                    )
            for at, top, part in parts:
                new = jnp.where(rows == at, jnp.maximum(peak, top), peak)
                total = total * jnp.exp2(peak - new) + jnp.where(
                    rows == at, part * jnp.exp2(top - new), 0.0
                )
                peak = new
            return peak, total

        init = (jnp.full((SIDE, BLK), NEG, F32), jnp.zeros((SIDE, BLK), F32))
        return lax.fori_loop(0, cap // step, body, init)

    def joined(peak, total):
        return jnp.where(total > 0, peak + log2(jnp.maximum(total, 1e-30)), NEG)

    def merge(buf, it, n):
        top = buf[it, 0]
        for k in range(1, n):
            top = jnp.maximum(top, buf[it, k])
        total = jnp.exp2(buf[it, 0] - top)
        for k in range(1, n):
            total = total + jnp.exp2(buf[it, k] - top)
        return top + log2(total)

    def cell_start(it, feats):
        peak, total = half(crosst, 1, 0, feats)
        buf_e[it, eme] = joined(peak, total)
        for _, dev, _, _ in e_peers:
            send(buf_e.at[it, eme], buf_e.at[it, eme], sem_e.at[0, it], sem_e.at[1, it], dev)
        return peak, total

    def cell_end(it):
        wait_for(buf_e.at[it, pl.ds(0, 15)], sem_e.at[1, it])
        pot = cell_log - merge(buf_e, it, 16)
        lane_spread(pot, spread)
        return pot

    def iteration(it, _):
        cell_start(it, None)
        cell_end(it)
        peak, total = half(cross, 0, 1, None)
        buf_d[it, dme] = joined(peak, total)
        for _, dev, _ in d_peers:
            send(buf_d.at[it, dme], buf_d.at[it, dme], sem_d.at[0, it], sem_d.at[1, it], dev)
        wait_for(buf_d.at[it, pl.ds(0, 7)], sem_d.at[1, it])
        lane_spread(spot_log - merge(buf_d, it, 8), spread)
        return 0

    lax.fori_loop(0, ITERS - 1, iteration, 0)

    wait_for(flag_e.at[pl.ds(0, 15)], sem_e.at[1, ITERS])
    over = flag_e[0]
    for k in range(1, 16):
        over = jnp.maximum(over, flag_e[k])
    flag_d[dme] = over
    for _, dev, _ in d_peers:
        send(flag_d.at[dme], flag_d.at[dme], sem_d.at[0, ITERS], sem_d.at[1, ITERS], dev)

    def gather_maps(peak, total, msg, transposed):
        peak_scr[...] = peak
        blockmap[cap] = jnp.zeros((FEAT, BLK), F32)
        slot_peak[cap] = jnp.full((1, BLK), NEG, F32)

        def one(b, _):
            top = peak_scr[pl.ds(b, 1), :]
            acc = jnp.zeros((FEAT, BLK), F32)
            for k in range(SIDE):
                e = tab_s[k, core * SIDE + b] if transposed else tab_s[b, core * SIDE + k]
                e = within(e, cap)
                acc = acc + blockmap[e] * jnp.exp2(slot_peak[e] - top)
            msg[b, pl.ds(0, FEAT), :] = acc
            return 0

        lax.fori_loop(0, SIDE, one, 0)
        for b in range(SIDE):
            msg[b, pl.ds(FEAT, 8), :] = jnp.concatenate(
                [peak[b : b + 1], total[b : b + 1], jnp.zeros((6, BLK), F32)], axis=0
            )

    def total_map(take, n):
        top = take(0, pl.ds(FEAT, 8))[0:1]
        for k in range(1, n):
            top = jnp.maximum(top, take(k, pl.ds(FEAT, 8))[0:1])
        total = jnp.zeros((1, BLK), F32)
        acc = jnp.zeros((FEAT, BLK), F32)
        for k in range(n):
            stat = take(k, pl.ds(FEAT, 8))
            scale = jnp.exp2(stat[0:1] - top)
            total = total + stat[1:2] * scale
            acc = acc + take(k, pl.ds(0, FEAT)) * scale
        return top + log2(total), acc / total

    peak, total = cell_start(ITERS - 1, shh)
    gather_maps(peak, total, msg_c, False)
    for _, dev, s2, k2 in e_peers:
        send(msg_c.at[k2 * 8 + s2], rcv_c.at[eme], sem_map.at[0], sem_map.at[1], dev)
    rcv_c[eme] = msg_c[core * 8 + si]
    cell_pot = cell_end(ITERS - 1)

    peak, total = half(cross, 0, 1, chh)
    gather_maps(peak, total, msg_s, True)
    for _, dev, d2 in d_peers:
        send(msg_s.at[pl.ds(d2 * 2, 2)], rcv_s.at[dme], sem_map.at[2], sem_map.at[3], dev)
    rcv_s[dme] = msg_s[pl.ds(dme * 2, 2)]

    wait_for(rcv_c.at[pl.ds(0, 15)], sem_map.at[1])
    _, block = total_map(lambda k, r: rcv_c[k, r, :], 16)
    own_c[...] = block
    at = pl.ds(pl.multiple_of(si * BLK, BLK), BLK)
    cmap_out[:, at] = block
    for a in range(2):
        for b in (2, 1, 3, 0):
            if a or b:
                s2 = lax.rem(yhi + a, 2) * 4 + lax.rem(zz + b, 4)
                send(own_c, cmap_out.at[:, at], sem_map.at[4], sem_map.at[5], (ci, s2))

    wait_for(rcv_s.at[pl.ds(0, 7)], sem_map.at[3])
    lses = []
    for h in range(2):
        lse, block = total_map(lambda k, r: rcv_s[k, h, r, :], 8)
        own_s[:, pl.ds(h * BLK, BLK)] = block
        lses.append(lse)
    pot_s[dme] = jnp.concatenate(lses + [jnp.zeros((6, BLK), F32)], axis=0)
    half_at = core * SIDE * BLK
    at = pl.ds(pl.multiple_of(half_at + dme * 2 * BLK, 2 * BLK), 2 * BLK)
    smap_out[:, at] = own_s[...]
    for _, dev, _ in d_peers:
        send(pot_s.at[dme], pot_s.at[dme], sem_map.at[6], sem_map.at[7], dev)
        send(own_s, smap_out.at[:, at], sem_map.at[8], sem_map.at[9], dev)

    cell_norm = jnp.zeros((8, BLK), F32)
    rows8 = lax.broadcasted_iota(jnp.int32, (8, BLK), 0)
    for b in range(8):
        wide = swap_out[b]
        cell_norm = jnp.where(
            rows8 == b, jnp.sum(wide * wide, axis=0, keepdims=True) * NORM, cell_norm
        )
    cell_own = jnp.where(first, cell_pot[0:8], cell_pot[8:16])
    cpot_out[...] = (cell_own + cell_norm) * (1.0 / UNIT)

    wait_for(pot_s.at[pl.ds(0, 7)], sem_map.at[7])
    lse = jnp.concatenate([pot_s[k, 0:2, :] for k in range(8)], axis=0)
    half_rows = pl.ds(pl.multiple_of(core * SIDE, SIDE), SIDE)
    spot_out[half_rows, :] = (spot_log - lse + spot_norm) * (1.0 / UNIT)
    send(spot_out.at[half_rows], spot_out.at[half_rows], sem_swap.at[4], sem_swap.at[5], partner)
    half_cols = pl.ds(pl.multiple_of(half_at, SIDE * BLK), SIDE * BLK)
    part = smap_out.at[:, pl.ds(0, 7 * 2 * BLK)]
    wait_for(part, sem_map.at[9])
    send(smap_out.at[:, half_cols], smap_out.at[:, half_cols], sem_swap.at[6], sem_swap.at[7], partner)

    wait_for(flag_d.at[pl.ds(0, 7)], sem_d.at[1, ITERS])
    over = flag_d[0]
    for k in range(1, 8):
        over = jnp.maximum(over, flag_d[k])
    flag_out[...] = over

    wait_for(cmap_out.at[:, pl.ds(0, 7 * BLK)], sem_map.at[5])
    wait_for(spot_out.at[pl.ds(0, SIDE)], sem_swap.at[5])
    wait_for(smap_out.at[:, pl.ds(0, SIDE * BLK)], sem_swap.at[7])
    wait_for(side_out, sem_swap.at[0])
    wait_for(swap_out, sem_swap.at[2])
    wait_for(spot_out.at[pl.ds(0, SIDE)], sem_swap.at[4])
    wait_for(smap_out.at[:, pl.ds(0, SIDE * BLK)], sem_swap.at[6])
    wait_for(rcv_c.at[pl.ds(0, 15)], sem_map.at[0])
    wait_for(rcv_s.at[pl.ds(0, 7)], sem_map.at[2])
    wait_for(cmap_out.at[:, pl.ds(0, 7 * BLK)], sem_map.at[4])
    wait_for(pot_s.at[pl.ds(0, 7)], sem_map.at[6])
    wait_for(part, sem_map.at[8])
    wait_for(flag_e.at[pl.ds(0, 15)], sem_e.at[0, ITERS])
    wait_for(flag_d.at[pl.ds(0, 7)], sem_d.at[0, ITERS])

    def sent(it, _):
        wait_for(buf_e.at[it, pl.ds(0, 15)], sem_e.at[0, it])
        wait_for(buf_d.at[it, pl.ds(0, 7)], sem_d.at[0, it])
        return 0

    lax.fori_loop(0, ITERS - 1, sent, 0)
    wait_for(buf_e.at[ITERS - 1, pl.ds(0, 15)], sem_e.at[0, ITERS - 1])


def run(cap, collective, cfeat, sfeat, cmass, smass, pattern):
    width = 128 if cap <= 128 else 256
    vmem = lambda *shape: pltpu.VMEM(shape, F32)
    half = lambda *shape: pltpu.VMEM(shape, BF16)
    shape = lambda *dims: jax.ShapeDtypeStruct(dims, F32)
    scratch = [
        vmem(8, FEAT, BLK), vmem(8, FEAT, BLK), vmem(2, 8, BLK), vmem(2, 8, BLK),
        half(SIDE, FEAT, BLK), half(SIDE, BLK, FEAT), half(SIDE, FEAT, BLK), half(SIDE, BLK, FEAT),
        vmem(cap, BLK, BLK), vmem(cap, BLK, BLK), vmem(SIDE, BLK, BLK),
        vmem(cap + 1, FEAT, BLK), vmem(cap + 1, 1, BLK), vmem(SIDE, BLK),
        pltpu.VMEM((8, width), jnp.int32), pltpu.SMEM((8, width), jnp.int32),
        pltpu.VMEM((SIDE, BLK), jnp.int32), pltpu.SMEM((SIDE, BLK), jnp.int32),
        vmem(ITERS, 16, SIDE, BLK), vmem(ITERS - 1, 8, SIDE, BLK), vmem(16, 8, BLK), vmem(8, 8, BLK),
        vmem(SIDE, MSG, BLK), vmem(16, MSG, BLK), vmem(SIDE, MSG, BLK), vmem(8, 2, MSG, BLK),
        vmem(FEAT, BLK), vmem(FEAT, 2 * BLK), vmem(8, 8, BLK),
        pltpu.SemaphoreType.DMA((8,)), pltpu.SemaphoreType.DMA((2, ITERS + 1)),
        pltpu.SemaphoreType.DMA((2, ITERS + 1)), pltpu.SemaphoreType.DMA((10,)),
        pltpu.SemaphoreType.DMA((2,)),
    ]
    return pl.pallas_call(
        functools.partial(sinkhorn_kernel, cap),
        out_shape=(shape(8, BLK), shape(32, BLK), shape(FEAT, 1024), shape(FEAT, 4096), shape(8, BLK)),
        in_specs=[pl.BlockSpec(memory_space=pltpu.VMEM)] * 5,
        out_specs=tuple([pl.BlockSpec(memory_space=pltpu.VMEM)] * 5),
        scratch_shapes=scratch,
        compiler_params=pltpu.CompilerParams(
            collective_id=collective, has_side_effects=True, vmem_limit_bytes=60 * 2**20
        ),
    )(cfeat, sfeat, cmass, smass, pattern)


def per_device(cell_feat, spot_feat, cell_mass, spot_mass, block_pattern):
    args = (cell_feat.T, spot_feat.T, cell_mass.reshape(8, BLK), spot_mass.reshape(32, BLK), block_pattern)
    outs = run(56, 0, *args)
    cpot, spot, cmap, smap, _ = lax.while_loop(
        lambda now: now[4][0, 0] > 0, lambda now: run(SIDE * SIDE, 1, *args), outs
    )
    return cpot.reshape(1024), spot.reshape(4096), cmap.T, smap.T


def solution(mesh):
    in_specs = (P("cells", None), P("spots", None), P("cells"), P("spots"), P("cells", "spots"))
    out_specs = (P("cells"), P("spots"), P("cells", None), P("spots", None))
    return jax.shard_map(
        per_device, mesh=mesh, in_specs=in_specs, out_specs=out_specs, check_vma=False
    )
```

```python
import functools
import math

import jax
import jax.numpy as jnp
from jax import lax
from jax.experimental import pallas as pl
from jax.experimental.pallas import tpu as pltpu
from jax.sharding import PartitionSpec as P

FEAT = 64
BLK = 128
ITERS = 5
EPSILON = 0.05
NEG = -1e30
LOG2E = math.log2(math.e)
UNIT = LOG2E / EPSILON
CROSS = UNIT * 2.0 / FEAT
NORM = UNIT / FEAT
SIDE = 16
GAP = 90.0
MSG = FEAT + 8
MESH = pl.DeviceIdType.MESH
F32 = jnp.float32
BF16 = jnp.bfloat16


def log2(v):
    return jnp.log(v) * LOG2E


def wait_for(view, sem):
    pltpu.make_async_copy(view, view, sem).wait()


def send(src, dst, ssem, rsem, dev):
    pltpu.make_async_remote_copy(
        src_ref=src, dst_ref=dst, send_sem=ssem, recv_sem=rsem, device_id=dev, device_id_type=MESH
    ).start()


def within(index, top):
    return jnp.minimum(jnp.maximum(index, 0), top)


def ring(offset):
    return {0: 0, 1: 1, 2: 2, 3: 1}[offset]


def lane_spread(pot, out):
    full = jnp.concatenate([pot, jnp.zeros((BLK - SIDE, BLK), F32)], axis=0)
    turned = jnp.transpose(full)
    for b in range(SIDE):
        out[b] = jnp.broadcast_to(turned[:, b : b + 1], (BLK, BLK))


def sinkhorn_kernel(
    cap, quick, cfeat_h, sfeat_h, cmass_h, smass_h, pattern_h,
    cpot_out, spot_out, cmap_out, smap_out, flag_out,
    cfeat, sfeat, cmass, smass, pattern, swap_out, swap_in, side_out, side_in, chh, cht, shh, sht, cross, crosst, spread,
    blockmap, slot_peak, peak_scr, list_v, list_s, tab_v, tab_s,
    buf_e, buf_d, flag_e, flag_d, msg_c, rcv_c, msg_s, rcv_s, own_c, own_s, pot_s,
    sem_swap, sem_e, sem_d, sem_map, sem_loc, sem_in, *more,
):
    ci = lax.axis_index("cells")
    si = lax.axis_index("spots")
    core = ci % 2
    dme = ci // 2
    ylo, xx = dme // 4, dme % 4
    yhi, zz = si // 4, si % 4
    eme = si * 2 + core
    partner = (ci + 1 - 2 * core, si)

    e_peers = []
    for a in range(2):
        for b in range(4):
            for k in range(2):
                if a or b or k:
                    s2 = lax.rem(yhi + a, 2) * 4 + lax.rem(zz + b, 4)
                    k2 = lax.rem(core + k, 2)
                    e_peers.append((2 * a + ring(b) + 0.1 * k, (dme * 2 + k2, s2), s2, k2))
    e_peers.sort(key=lambda item: -item[0])
    d_peers = []
    for a in range(2):
        for b in range(4):
            if a or b:
                d2 = lax.rem(ylo + a, 2) * 4 + lax.rem(xx + b, 4)
                d_peers.append((a + ring(b), (d2 * 2 + core, si), d2))
    d_peers.sort(key=lambda item: -item[0])

    if quick:
        weight_c, weight_s, bound_c, bound_s, worst = more

    barrier = pltpu.get_barrier_semaphore()
    for item in e_peers + d_peers:
        pl.semaphore_signal(barrier, inc=1, device_id=item[1], device_id_type=MESH)

    loads = [
        pltpu.make_async_copy(src, dst, sem_in.at[k])
        for k, (src, dst) in enumerate(
            ((cfeat_h, cfeat), (sfeat_h, sfeat), (cmass_h, cmass), (smass_h, smass), (pattern_h, pattern))
        )
    ]
    for load in loads:
        load.start()
    for load in loads:
        load.wait()

    def own_cells(b, _):
        block = cfeat[:, pl.ds(pl.multiple_of(b * BLK, BLK), BLK)]
        wide = block.astype(F32)
        swap_out[b] = wide
        chh[core * 8 + b] = block
        cht[core * 8 + b] = jnp.transpose(wide).astype(BF16)
        return 0

    lax.fori_loop(0, 8, own_cells, 0)

    def own_spots(b, norms):
        block = sfeat[:, pl.ds(pl.multiple_of((core * SIDE + b) * BLK, BLK), BLK)]
        wide = block.astype(F32)
        shh[b] = block
        sht[b] = jnp.transpose(wide).astype(BF16)
        here = lax.broadcasted_iota(jnp.int32, (SIDE, BLK), 0) == b
        return jnp.where(here, jnp.sum(wide * wide, axis=0, keepdims=True) * NORM, norms)

    spot_norm = lax.fori_loop(0, SIDE, own_spots, jnp.zeros((SIDE, BLK), F32))
    pattern_own = (pattern[...] > 0).astype(F32)
    side_out[0] = cmass[...]
    side_out[1] = jnp.concatenate([pattern_own, jnp.zeros((8, BLK - 32), F32)], axis=1)

    pl.semaphore_wait(barrier, len(e_peers) + len(d_peers))

    send(side_out, side_in, sem_swap.at[0], sem_swap.at[1], partner)
    send(swap_out, swap_in, sem_swap.at[2], sem_swap.at[3], partner)
    wait_for(side_in, sem_swap.at[1])

    first = core == 0
    mine, theirs = side_out[1], side_in[1]
    lane = lax.broadcasted_iota(jnp.int32, (SIDE, BLK), 1)
    both = jnp.concatenate(
        [jnp.where(first, mine, theirs), jnp.where(first, theirs, mine)], axis=0
    )
    both = jnp.where((lane >= core * SIDE) & (lane < core * SIDE + SIDE), both, 0.0)
    upto = (
        lax.broadcasted_iota(jnp.int32, (BLK, BLK), 0)
        < lax.broadcasted_iota(jnp.int32, (BLK, BLK), 1)
    ).astype(BF16)
    inside = jnp.dot(both.astype(BF16), upto, preferred_element_type=F32)
    per_row = jnp.broadcast_to(jnp.sum(both, axis=1, keepdims=True), (SIDE, BLK))
    earlier = (
        lax.broadcasted_iota(jnp.int32, (SIDE, SIDE), 1)
        < lax.broadcasted_iota(jnp.int32, (SIDE, SIDE), 0)
    ).astype(BF16)
    before = jnp.dot(earlier, per_row.astype(BF16), preferred_element_type=F32)
    place = jnp.where(both > 0, before + inside, -1.0)
    count = jnp.sum(jnp.sum(both, axis=1, keepdims=True), axis=0, keepdims=True)
    over = jnp.broadcast_to(jnp.where(count > cap, 1.0, 0.0), (8, BLK))
    width = list_v.shape[1]
    pairs = SIDE * SIDE
    wide_place = jnp.broadcast_to(place[:, None, :], (SIDE, SIDE, BLK)).reshape(pairs, BLK)
    pair = lax.broadcasted_iota(jnp.int32, (pairs, BLK), 0)
    pair_lane = lax.broadcasted_iota(jnp.int32, (pairs, BLK), 1)
    chosen = pair_lane == core * SIDE + pair % SIDE
    slot_of = jnp.sum(jnp.where(chosen, wide_place, 0.0), axis=1, keepdims=True)
    hot = slot_of == lax.broadcasted_iota(jnp.int32, (pairs, width), 1).astype(F32)
    kind = lax.broadcasted_iota(jnp.int32, (8, pairs), 0)
    which = lax.broadcasted_iota(jnp.int32, (8, pairs), 1)
    facts = jnp.where(kind == 0, which // SIDE, jnp.where(kind == 1, which % SIDE, 1))
    lists = jnp.dot(
        facts.astype(F32).astype(BF16), hot.astype(F32).astype(BF16), preferred_element_type=F32
    )
    none = 99.0 * (1.0 - lists[2:3])
    kind = lax.broadcasted_iota(jnp.int32, (8, width), 0)
    lists = jnp.where(kind >= 2, 0.0, lists) + jnp.where(
        kind == 2, lists[0:1] + none, jnp.where(kind == 3, lists[1:2] + none, 0.0)
    )
    list_v[...] = lists.astype(jnp.int32)
    tab_v[...] = jnp.where((place < 0) | (place >= cap), float(cap), place).astype(jnp.int32)
    copies = [
        pltpu.make_async_copy(list_v, list_s, sem_loc.at[0]),
        pltpu.make_async_copy(tab_v, tab_s, sem_loc.at[1]),
    ]
    for copy in copies:
        copy.start()

    cell_log = log2(
        jnp.concatenate(
            [
                jnp.where(first, side_out[0], side_in[0]),
                jnp.where(first, side_in[0], side_out[0]),
            ],
            axis=0,
        )
    )
    spot_log = log2(smass[pl.ds(pl.multiple_of(core * SIDE, SIDE), SIDE), :])

    lane_spread(-spot_norm, spread)
    wait_for(swap_in, sem_swap.at[3])

    def other_cells(b, _):
        wide = swap_in[b]
        chh[(1 - core) * 8 + b] = wide.astype(BF16)
        cht[(1 - core) * 8 + b] = jnp.transpose(wide).astype(BF16)
        return 0

    lax.fori_loop(0, 8, other_cells, 0)
    for copy in copies:
        copy.wait()

    step = 13 if quick else 8

    def build(i, _):
        for k in range(step):
            e = i * step + k
            r = within(list_s[0, e], SIDE - 1)
            c = within(list_s[1, e], SIDE - 1)
            cross[e] = jnp.dot(cht[r], shh[c], preferred_element_type=F32) * CROSS
            crosst[e] = jnp.dot(sht[c], chh[r], preferred_element_type=F32) * CROSS
        return 0

    lax.fori_loop(0, cap // step, build, 0)

    rows = lax.broadcasted_iota(jnp.int32, (SIDE, BLK), 0)

    def half(scores, other, own, feats):
        def body(i, carry):
            peak, total = carry
            parts = []
            for k in range(step):
                e = i * step + k
                o = within(list_s[other, e], SIDE - 1)
                v = scores[e] + spread[o]
                top = jnp.max(v, axis=0, keepdims=True)
                p = jnp.exp2(v - top)
                parts.append((list_s[own + 2, e], top, jnp.sum(p, axis=0, keepdims=True)))
                if feats is not None:
                    slot_peak[e] = top
                    blockmap[e] = jnp.dot(
                        feats[o], p.astype(BF16), preferred_element_type=F32
                    )
            for at, top, part in parts:
                new = jnp.where(rows == at, jnp.maximum(peak, top), peak)
                total = total * jnp.exp2(peak - new) + jnp.where(
                    rows == at, part * jnp.exp2(top - new), 0.0
                )
                peak = new
            return peak, total

        init = (jnp.full((SIDE, BLK), NEG, F32), jnp.zeros((SIDE, BLK), F32))
        return lax.fori_loop(0, cap // step, body, init)

    def joined(peak, total):
        return jnp.where(total > 0, peak + log2(jnp.maximum(total, 1e-30)), NEG)

    def merge(buf, it, n):
        top = buf[it, 0]
        for k in range(1, n):
            top = jnp.maximum(top, buf[it, k])
        total = jnp.exp2(buf[it, 0] - top)
        for k in range(1, n):
            total = total + jnp.exp2(buf[it, k] - top)
        return top + log2(total)

    def cell_send(it, value):
        buf_e[it, eme] = value
        for _, dev, _, _ in e_peers:
            send(buf_e.at[it, eme], buf_e.at[it, eme], sem_e.at[0, it], sem_e.at[1, it], dev)

    def cell_merge(it):
        wait_for(buf_e.at[it, pl.ds(0, 15)], sem_e.at[1, it])
        return merge(buf_e, it, 16)

    def spot_exchange(it, value):
        buf_d[it, dme] = value
        for _, dev, _ in d_peers:
            send(buf_d.at[it, dme], buf_d.at[it, dme], sem_d.at[0, it], sem_d.at[1, it], dev)
        wait_for(buf_d.at[it, pl.ds(0, 7)], sem_d.at[1, it])
        return merge(buf_d, it, 8)

    def peaks(i, carry):
        top_c, top_s = carry
        for k in range(step):
            e = i * step + k
            one = jnp.max(crosst[e], axis=0, keepdims=True)
            two = jnp.max(cross[e], axis=0, keepdims=True)
            top_c = jnp.where(rows == list_s[2, e], jnp.maximum(top_c, one), top_c)
            top_s = jnp.where(rows == list_s[3, e], jnp.maximum(top_s, two), top_s)
        return top_c, top_s

    def weights(i, _):
        for k in range(step):
            e = i * step + k
            r = within(list_s[0, e], SIDE - 1)
            c = within(list_s[1, e], SIDE - 1)
            weight_c[e] = jnp.exp2(crosst[e] - bound_c[pl.ds(r, 1), :])
            weight_s[e] = jnp.exp2(cross[e] - bound_s[pl.ds(c, 1), :])
        return 0

    def quick_half(weight, bound, pot, other, own):
        most = jnp.max(jnp.max(pot, axis=0, keepdims=True), axis=1, keepdims=True)
        lane_spread(jnp.exp2(pot - most), spread)

        def body(i, total):
            parts = []
            for k in range(step):
                e = i * step + k
                o = within(list_s[other, e], SIDE - 1)
                parts.append(
                    (list_s[own + 2, e], jnp.sum(weight[e] * spread[o], axis=0, keepdims=True))
                )
            for at, part in parts:
                total = total + jnp.where(rows == at, part, 0.0)
            return total

        total = lax.fori_loop(0, cap // step, body, jnp.zeros((SIDE, BLK), F32))
        top = bound[...] + most
        return top, jnp.where(total > 0, top + log2(jnp.maximum(total, 1e-38)), NEG)

    def watch(top, lse):
        worst[...] = jnp.where(top - lse <= GAP, worst[...], 1.0)

    def quick_spots(it, cell_lse):
        top, value = quick_half(weight_s, bound_s, cell_log - cell_lse, 0, 1)
        lse = spot_exchange(it, value)
        watch(top, lse)
        return spot_log - lse

    def first_steps():
        peak, total = half(crosst, 1, 0, None)
        cell_send(0, joined(peak, total))
        init = jnp.full((SIDE, BLK), NEG, F32)
        top_c, top_s = lax.fori_loop(0, cap // step, peaks, (init, init))
        bound_c[...] = top_c
        bound_s[...] = top_s
        worst[...] = jnp.zeros((SIDE, BLK), F32)
        lax.fori_loop(0, cap // step, weights, 0)

        def iteration(it, lse):
            pot = quick_spots(it, lse)
            top, value = quick_half(weight_c, bound_c, pot, 1, 0)
            cell_send(it + 1, value)
            lse = cell_merge(it + 1)
            watch(top, lse)
            return lse

        lse = lax.fori_loop(0, ITERS - 2, iteration, cell_merge(0))
        lane_spread(quick_spots(ITERS - 2, lse), spread)
        return jnp.max(worst[...], axis=0, keepdims=True)

    def first_steps_whole():
        def iteration(it, _):
            peak, total = half(crosst, 1, 0, None)
            cell_send(it, joined(peak, total))
            lane_spread(cell_log - cell_merge(it), spread)
            peak, total = half(cross, 0, 1, None)
            lane_spread(spot_log - spot_exchange(it, joined(peak, total)), spread)
            return 0

        lax.fori_loop(0, ITERS - 1, iteration, 0)
        return jnp.zeros((1, BLK), F32)

    over = jnp.maximum(over, first_steps() if quick else first_steps_whole())

    def gather_maps(peak, total, msg, transposed):
        peak_scr[...] = peak
        blockmap[cap] = jnp.zeros((FEAT, BLK), F32)
        slot_peak[cap] = jnp.full((1, BLK), NEG, F32)

        def one(b, _):
            top = peak_scr[pl.ds(b, 1), :]
            acc = jnp.zeros((FEAT, BLK), F32)
            for k in range(SIDE):
                e = tab_s[k, core * SIDE + b] if transposed else tab_s[b, core * SIDE + k]
                e = within(e, cap)
                acc = acc + blockmap[e] * jnp.exp2(slot_peak[e] - top)
            msg[b, pl.ds(0, FEAT), :] = acc
            return 0

        lax.fori_loop(0, SIDE, one, 0)
        for b in range(SIDE):
            msg[b, pl.ds(FEAT, 8), :] = jnp.concatenate(
                [peak[b : b + 1], total[b : b + 1], jnp.zeros((6, BLK), F32)], axis=0
            )

    def total_map(take, n):
        top = take(0, pl.ds(FEAT, 8))[0:1]
        for k in range(1, n):
            top = jnp.maximum(top, take(k, pl.ds(FEAT, 8))[0:1])
        total = jnp.zeros((1, BLK), F32)
        acc = jnp.zeros((FEAT, BLK), F32)
        for k in range(n):
            stat = take(k, pl.ds(FEAT, 8))
            scale = jnp.exp2(stat[0:1] - top)
            total = total + stat[1:2] * scale
            acc = acc + take(k, pl.ds(0, FEAT)) * scale
        return top + log2(total), acc / total

    peak, total = half(crosst, 1, 0, shh)
    cell_send(ITERS - 1, joined(peak, total))
    flag_e[eme] = over
    for _, dev, _, _ in e_peers:
        send(flag_e.at[eme], flag_e.at[eme], sem_e.at[0, ITERS], sem_e.at[1, ITERS], dev)
    gather_maps(peak, total, msg_c, False)
    for _, dev, s2, k2 in e_peers:
        send(msg_c.at[k2 * 8 + s2], rcv_c.at[eme], sem_map.at[0], sem_map.at[1], dev)
    rcv_c[eme] = msg_c[core * 8 + si]
    cell_pot = cell_log - cell_merge(ITERS - 1)
    lane_spread(cell_pot, spread)

    peak, total = half(cross, 0, 1, chh)
    gather_maps(peak, total, msg_s, True)
    for _, dev, d2 in d_peers:
        send(msg_s.at[pl.ds(d2 * 2, 2)], rcv_s.at[dme], sem_map.at[2], sem_map.at[3], dev)
    rcv_s[dme] = msg_s[pl.ds(dme * 2, 2)]

    wait_for(flag_e.at[pl.ds(0, 15)], sem_e.at[1, ITERS])
    over = flag_e[0]
    for k in range(1, 16):
        over = jnp.maximum(over, flag_e[k])
    flag_d[dme] = over
    for _, dev, _ in d_peers:
        send(flag_d.at[dme], flag_d.at[dme], sem_d.at[0, ITERS], sem_d.at[1, ITERS], dev)

    wait_for(rcv_c.at[pl.ds(0, 15)], sem_map.at[1])
    _, block = total_map(lambda k, r: rcv_c[k, r, :], 16)
    own_c[...] = block
    at = pl.ds(pl.multiple_of(si * BLK, BLK), BLK)
    cmap_out[:, at] = block
    for a in range(2):
        for b in (2, 1, 3, 0):
            if a or b:
                s2 = lax.rem(yhi + a, 2) * 4 + lax.rem(zz + b, 4)
                send(own_c, cmap_out.at[:, at], sem_map.at[4], sem_map.at[5], (ci, s2))

    wait_for(rcv_s.at[pl.ds(0, 7)], sem_map.at[3])
    lses = []
    for h in range(2):
        lse, block = total_map(lambda k, r: rcv_s[k, h, r, :], 8)
        own_s[:, pl.ds(h * BLK, BLK)] = block
        lses.append(lse)
    pot_s[dme] = jnp.concatenate(lses + [jnp.zeros((6, BLK), F32)], axis=0)
    half_at = core * SIDE * BLK
    at = pl.ds(pl.multiple_of(half_at + dme * 2 * BLK, 2 * BLK), 2 * BLK)
    smap_out[:, at] = own_s[...]
    for _, dev, _ in d_peers:
        send(pot_s.at[dme], pot_s.at[dme], sem_map.at[6], sem_map.at[7], dev)
        send(own_s, smap_out.at[:, at], sem_map.at[8], sem_map.at[9], dev)

    cell_norm = jnp.zeros((8, BLK), F32)
    rows8 = lax.broadcasted_iota(jnp.int32, (8, BLK), 0)
    for b in range(8):
        wide = swap_out[b]
        cell_norm = jnp.where(
            rows8 == b, jnp.sum(wide * wide, axis=0, keepdims=True) * NORM, cell_norm
        )
    cell_own = jnp.where(first, cell_pot[0:8], cell_pot[8:16])
    cpot_out[...] = (cell_own + cell_norm) * (1.0 / UNIT)

    wait_for(pot_s.at[pl.ds(0, 7)], sem_map.at[7])
    lse = jnp.concatenate([pot_s[k, 0:2, :] for k in range(8)], axis=0)
    half_rows = pl.ds(pl.multiple_of(core * SIDE, SIDE), SIDE)
    spot_out[half_rows, :] = (spot_log - lse + spot_norm) * (1.0 / UNIT)
    send(spot_out.at[half_rows], spot_out.at[half_rows], sem_swap.at[4], sem_swap.at[5], partner)
    half_cols = pl.ds(pl.multiple_of(half_at, SIDE * BLK), SIDE * BLK)
    part = smap_out.at[:, pl.ds(0, 7 * 2 * BLK)]
    wait_for(part, sem_map.at[9])
    send(smap_out.at[:, half_cols], smap_out.at[:, half_cols], sem_swap.at[6], sem_swap.at[7], partner)

    wait_for(flag_d.at[pl.ds(0, 7)], sem_d.at[1, ITERS])
    over = flag_d[0]
    for k in range(1, 8):
        over = jnp.maximum(over, flag_d[k])
    flag_out[0] = jnp.max(over).astype(jnp.int32)

    wait_for(cmap_out.at[:, pl.ds(0, 7 * BLK)], sem_map.at[5])
    wait_for(spot_out.at[pl.ds(0, SIDE)], sem_swap.at[5])
    wait_for(smap_out.at[:, pl.ds(0, SIDE * BLK)], sem_swap.at[7])
    wait_for(side_out, sem_swap.at[0])
    wait_for(swap_out, sem_swap.at[2])
    wait_for(spot_out.at[pl.ds(0, SIDE)], sem_swap.at[4])
    wait_for(smap_out.at[:, pl.ds(0, SIDE * BLK)], sem_swap.at[6])
    wait_for(rcv_c.at[pl.ds(0, 15)], sem_map.at[0])
    wait_for(rcv_s.at[pl.ds(0, 7)], sem_map.at[2])
    wait_for(cmap_out.at[:, pl.ds(0, 7 * BLK)], sem_map.at[4])
    wait_for(pot_s.at[pl.ds(0, 7)], sem_map.at[6])
    wait_for(part, sem_map.at[8])
    wait_for(flag_e.at[pl.ds(0, 15)], sem_e.at[0, ITERS])
    wait_for(flag_d.at[pl.ds(0, 7)], sem_d.at[0, ITERS])

    def sent(it, _):
        wait_for(buf_e.at[it, pl.ds(0, 15)], sem_e.at[0, it])
        wait_for(buf_d.at[it, pl.ds(0, 7)], sem_d.at[0, it])
        return 0

    lax.fori_loop(0, ITERS - 1, sent, 0)
    wait_for(buf_e.at[ITERS - 1, pl.ds(0, 15)], sem_e.at[0, ITERS - 1])


def run(cap, quick, collective, cfeat, sfeat, cmass, smass, pattern):
    width = 128 if cap <= 128 else 256
    vmem = lambda *shape: pltpu.VMEM(shape, F32)
    half = lambda *shape: pltpu.VMEM(shape, BF16)
    shape = lambda *dims: jax.ShapeDtypeStruct(dims, F32)
    scratch = [
        half(FEAT, 1024), half(FEAT, 4096), vmem(8, BLK), vmem(32, BLK), pltpu.VMEM((8, 32), jnp.int32),
        vmem(8, FEAT, BLK), vmem(8, FEAT, BLK), vmem(2, 8, BLK), vmem(2, 8, BLK),
        half(SIDE, FEAT, BLK), half(SIDE, BLK, FEAT), half(SIDE, FEAT, BLK), half(SIDE, BLK, FEAT),
        vmem(cap, BLK, BLK), vmem(cap, BLK, BLK), vmem(SIDE, BLK, BLK),
        vmem(cap + 1, FEAT, BLK), vmem(cap + 1, 1, BLK), vmem(SIDE, BLK),
        pltpu.VMEM((8, width), jnp.int32), pltpu.SMEM((8, width), jnp.int32),
        pltpu.VMEM((SIDE, BLK), jnp.int32), pltpu.SMEM((SIDE, BLK), jnp.int32),
        vmem(ITERS, 16, SIDE, BLK), vmem(ITERS - 1, 8, SIDE, BLK), vmem(16, 8, BLK), vmem(8, 8, BLK),
        vmem(SIDE, MSG, BLK), vmem(16, MSG, BLK), vmem(SIDE, MSG, BLK), vmem(8, 2, MSG, BLK),
        vmem(FEAT, BLK), vmem(FEAT, 2 * BLK), vmem(8, 8, BLK),
        pltpu.SemaphoreType.DMA((8,)), pltpu.SemaphoreType.DMA((2, ITERS + 1)),
        pltpu.SemaphoreType.DMA((2, ITERS + 1)), pltpu.SemaphoreType.DMA((10,)),
        pltpu.SemaphoreType.DMA((2,)), pltpu.SemaphoreType.DMA((5,)),
    ]
    if quick:
        scratch += [vmem(cap, BLK, BLK), vmem(cap, BLK, BLK)] + [vmem(SIDE, BLK)] * 3
    return pl.pallas_call(
        functools.partial(sinkhorn_kernel, cap, quick),
        out_shape=(shape(8, BLK), shape(32, BLK), shape(FEAT, 1024), shape(FEAT, 4096), jax.ShapeDtypeStruct((1,), jnp.int32)),
        in_specs=[pl.BlockSpec(memory_space=pltpu.HBM)] * 5,
        out_specs=tuple([pl.BlockSpec(memory_space=pltpu.VMEM)] * 4 + [pl.BlockSpec(memory_space=pltpu.SMEM)]),
        scratch_shapes=scratch,
        compiler_params=pltpu.CompilerParams(
            collective_id=collective, has_side_effects=True, vmem_limit_bytes=60 * 2**20
        ),
    )(cfeat, sfeat, cmass, smass, pattern)


def place_kernel(*refs):
    srcs, dsts, sems = refs[:4], refs[4:8], refs[8]
    copies = [pltpu.make_async_copy(s, d, sems.at[k]) for k, (s, d) in enumerate(zip(srcs, dsts))]
    for copy in copies:
        copy.start()
    for copy in copies:
        copy.wait()


def place(*arrays):
    return pl.pallas_call(
        place_kernel,
        out_shape=tuple(jax.ShapeDtypeStruct(a.shape, a.dtype) for a in arrays),
        in_specs=[pl.BlockSpec(memory_space=pl.ANY)] * 4,
        out_specs=tuple([pl.BlockSpec(memory_space=pl.ANY)] * 4),
        scratch_shapes=[pltpu.SemaphoreType.DMA((4,))],
    )(*arrays)


def per_device(cell_feat, spot_feat, cell_mass, spot_mass, block_pattern):
    args = (cell_feat.T, spot_feat.T, cell_mass.reshape(8, BLK), spot_mass.reshape(32, BLK), block_pattern)
    outs = run(52, True, 0, *args)
    cpot, spot, cmap, smap = lax.cond(
        outs[4][0] > 0, lambda now: place(*run(SIDE * SIDE, False, 1, *args)[:4]), lambda now: place(*now[:4]), outs
    )
    return cpot.reshape(1024), spot.reshape(4096), cmap.T, smap.T


def solution(mesh):
    in_specs = (P("cells", None), P("spots", None), P("cells"), P("spots"), P("cells", "spots"))
    out_specs = (P("cells"), P("spots"), P("cells", None), P("spots", None))
    return jax.shard_map(
        per_device, mesh=mesh, in_specs=in_specs, out_specs=out_specs, check_vma=False
    )
```

```python
import functools
import math

import jax
import jax.numpy as jnp
from jax import lax
from jax.experimental import pallas as pl
from jax.experimental.pallas import tpu as pltpu
from jax.sharding import PartitionSpec as P

FEAT = 64
BLK = 128
ITERS = 5
EPSILON = 0.05
NEG = -1e30
LOG2E = math.log2(math.e)
UNIT = LOG2E / EPSILON
CROSS = UNIT * 2.0 / FEAT
NORM = UNIT / FEAT
SIDE = 16
FIRST = 56
GAP = 90.0
DEEP = FEAT + 16
MSG = FEAT + 8
MESH = pl.DeviceIdType.MESH
F32 = jnp.float32
BF16 = jnp.bfloat16


def log2(v):
    return jnp.log(v) * LOG2E


def wait_for(view, sem):
    pltpu.make_async_copy(view, view, sem).wait()


def send(src, dst, ssem, rsem, dev):
    pltpu.make_async_remote_copy(
        src_ref=src, dst_ref=dst, send_sem=ssem, recv_sem=rsem, device_id=dev, device_id_type=MESH
    ).start()


def within(index, top):
    return jnp.minimum(jnp.maximum(index, 0), top)


def ring(offset):
    return {0: 0, 1: 1, 2: 2, 3: 1}[offset]


def lane_spread(pot, out):
    for b in range(SIDE):
        out[b] = jnp.transpose(jnp.broadcast_to(pot[b : b + 1], (BLK, BLK)))


def block_list(allowed, lane0, cols, width):
    rows = allowed.shape[0]
    upto = (
        lax.broadcasted_iota(jnp.int32, (BLK, BLK), 0)
        < lax.broadcasted_iota(jnp.int32, (BLK, BLK), 1)
    ).astype(BF16)
    inside = jnp.dot(allowed.astype(BF16), upto, preferred_element_type=F32)
    per_row = jnp.broadcast_to(jnp.sum(allowed, axis=1, keepdims=True), (rows, BLK))
    below = lax.broadcasted_iota(jnp.int32, (rows, BLK), 0)
    before = jnp.zeros((rows, BLK), F32)
    for r in range(rows - 1):
        before = before + jnp.where(below > r, per_row[r : r + 1], 0.0)
    place = jnp.where(allowed > 0, before + inside, -1.0)
    count = jnp.sum(jnp.sum(allowed, axis=1, keepdims=True), axis=0, keepdims=True)
    pairs = rows * cols
    wide_place = jnp.broadcast_to(place[:, None, :], (rows, cols, BLK)).reshape(pairs, BLK)
    pair = lax.broadcasted_iota(jnp.int32, (pairs, BLK), 0)
    pair_lane = lax.broadcasted_iota(jnp.int32, (pairs, BLK), 1)
    chosen = pair_lane == lane0 + pair % cols
    slot_of = jnp.sum(jnp.where(chosen, wide_place, 0.0), axis=1, keepdims=True)
    hot = slot_of == lax.broadcasted_iota(jnp.int32, (pairs, width), 1).astype(F32)
    kind = lax.broadcasted_iota(jnp.int32, (8, pairs), 0)
    which = lax.broadcasted_iota(jnp.int32, (8, pairs), 1)
    facts = jnp.where(kind == 0, which // cols, jnp.where(kind == 1, which % cols, 1))
    lists = jnp.dot(
        facts.astype(F32).astype(BF16), hot.astype(F32).astype(BF16), preferred_element_type=F32
    )
    none = 99.0 * (1.0 - lists[2:3])
    kind = lax.broadcasted_iota(jnp.int32, (8, width), 0)
    lists = jnp.where(kind >= 2, 0.0, lists) + jnp.where(
        kind == 2, lists[0:1] + none, jnp.where(kind == 3, lists[1:2] + none, 0.0)
    )
    return lists, place, count


def sinkhorn_kernel(
    cap, quick, cfeat_h, sfeat_h, cmass_h, smass_h, pattern_h,
    cpot_out, spot_out, cmap_out, smap_out, flag_out,
    cfeat, sfeat, cmass, smass, pattern, swap_out, swap_in, side_out, side_in, chh, cht, shh, sht, cross, crosst, spread,
    blockmap, slot_peak, peak_scr, list_v, list_s, tab_v, tab_s,
    buf_e, buf_d, flag_e, flag_d, msg_c, rcv_c, msg_s, rcv_s, own_c, own_s, pot_s,
    sem_swap, sem_e, sem_d, sem_map, sem_loc, sem_in, *more,
):
    ci = lax.axis_index("cells")
    si = lax.axis_index("spots")
    core = ci % 2
    dme = ci // 2
    ylo, xx = dme // 4, dme % 4
    yhi, zz = si // 4, si % 4
    eme = si * 2 + core
    partner = (ci + 1 - 2 * core, si)

    e_peers = []
    for a in range(2):
        for b in range(4):
            for k in range(2):
                if a or b or k:
                    s2 = lax.rem(yhi + a, 2) * 4 + lax.rem(zz + b, 4)
                    k2 = lax.rem(core + k, 2)
                    e_peers.append((2 * a + ring(b) + 0.1 * k, (dme * 2 + k2, s2), s2, k2))
    e_peers.sort(key=lambda item: -item[0])
    d_peers = []
    for a in range(2):
        for b in range(4):
            if a or b:
                d2 = lax.rem(ylo + a, 2) * 4 + lax.rem(xx + b, 4)
                d_peers.append((a + ring(b), (d2 * 2 + core, si), d2))
    d_peers.sort(key=lambda item: -item[0])

    if quick:
        weight_c, weight_s, bound_c, bound_s, worst, chx, list0_v, list0_s, buf_0 = more

    barrier = pltpu.get_barrier_semaphore()
    for item in e_peers + d_peers:
        pl.semaphore_signal(barrier, inc=1, device_id=item[1], device_id_type=MESH)

    loads = [
        pltpu.make_async_copy(src, dst, sem_in.at[k])
        for k, (src, dst) in enumerate(
            ((pattern_h, pattern), (cfeat_h, cfeat), (sfeat_h, sfeat), (cmass_h, cmass), (smass_h, smass))
        )
    ]
    for load in loads:
        load.start()
    loads[0].wait()
    pattern_own = (pattern[...] > 0).astype(F32)
    side_out[1] = jnp.concatenate([pattern_own, jnp.zeros((8, BLK - 32), F32)], axis=1)
    if quick:
        lists, _, count_0 = block_list(side_out[1], 0, 2 * SIDE, list0_v.shape[1])
        list0_v[...] = lists.astype(jnp.int32)
        copy_0 = pltpu.make_async_copy(list0_v, list0_s, sem_loc.at[2])
        copy_0.start()
    loads[1].wait()
    below = lax.broadcasted_iota(jnp.int32, (DEEP - FEAT, BLK), 0)

    def cells_turned(b, wide):
        cht[b] = jnp.transpose(wide).astype(BF16)

    def own_cells(i, _):
        for k in range(4):
            b = i * 4 + k
            block = cfeat[:, pl.ds(pl.multiple_of(b * BLK, BLK), BLK)]
            wide = block.astype(F32)
            swap_out[b] = wide
            chh[core * 8 + b] = block
            if quick:
                ones = jnp.where(below < 3, 1.0, 0.0).astype(BF16)
                chx[b] = jnp.concatenate([block, ones], axis=0)
            else:
                cells_turned(core * 8 + b, wide)
        return 0

    lax.fori_loop(0, 2, own_cells, 0)
    loads[2].wait()

    spots = 2 * SIDE if quick else SIDE
    offset = 0 if quick else core * SIDE
    mid = core * SIDE if quick else 0

    def own_spots(i, norms):
        for k in range(4):
            b = i * 4 + k
            block = sfeat[:, pl.ds(pl.multiple_of((offset + b) * BLK, BLK), BLK)]
            wide = block.astype(F32)
            norm = jnp.sum(wide * wide, axis=0, keepdims=True)
            shh[b] = block
            if quick:
                rest = norm * -0.5
                parts = jnp.zeros((DEEP - FEAT, BLK), F32)
                for n in range(3):
                    part = rest.astype(BF16).astype(F32)
                    parts = jnp.where(below == n, part, parts)
                    rest = rest - part
                wide = jnp.concatenate([wide, parts], axis=0)
            sht[b] = jnp.transpose(wide).astype(BF16)
            here = lax.broadcasted_iota(jnp.int32, (SIDE, BLK), 0) == b - mid
            norms = jnp.where(here, norm * NORM, norms)
        return norms

    spot_norm = lax.fori_loop(0, spots // 4, own_spots, jnp.zeros((SIDE, BLK), F32))

    def first_half():
        copy_0.wait()
        rows8 = lax.broadcasted_iota(jnp.int32, (8, BLK), 0)
        step = 14

        def body(i, carry):
            peak, total = carry
            parts = []
            for k in range(step):
                e = i * step + k
                r = within(list0_s[0, e], 7)
                c = within(list0_s[1, e], 2 * SIDE - 1)
                v = jnp.dot(sht[c], chx[r], preferred_element_type=F32) * CROSS
                top = jnp.max(v, axis=0, keepdims=True)
                part = jnp.sum(jnp.exp2(v - top), axis=0, keepdims=True)
                parts.append((list0_s[2, e], top, part))
            for at, top, part in parts:
                new = jnp.where(rows8 == at, jnp.maximum(peak, top), peak)
                total = total * jnp.exp2(peak - new) + jnp.where(
                    rows8 == at, part * jnp.exp2(top - new), 0.0
                )
                peak = new
            return peak, total

        init = (jnp.full((8, BLK), NEG, F32), jnp.zeros((8, BLK), F32))
        peak, total = lax.fori_loop(0, FIRST // step, body, init)
        buf_0[eme] = jnp.where(total > 0, peak + log2(jnp.maximum(total, 1e-30)), NEG)
        return jnp.where(count_0 > FIRST, 1.0, 0.0)

    over_0 = first_half() if quick else None
    pl.semaphore_wait(barrier, len(e_peers) + len(d_peers))
    loads[3].wait()
    loads[4].wait()
    side_out[0] = cmass[...]
    if quick:
        for _, dev, _, _ in e_peers:
            send(buf_0.at[eme], buf_0.at[eme], sem_e.at[0, 0], sem_e.at[1, 0], dev)

    send(side_out, side_in, sem_swap.at[0], sem_swap.at[1], partner)
    send(swap_out, swap_in, sem_swap.at[2], sem_swap.at[3], partner)
    wait_for(side_in, sem_swap.at[1])

    first = core == 0
    mine, theirs = side_out[1], side_in[1]
    lane = lax.broadcasted_iota(jnp.int32, (SIDE, BLK), 1)
    both = jnp.concatenate(
        [jnp.where(first, mine, theirs), jnp.where(first, theirs, mine)], axis=0
    )
    both = jnp.where((lane >= core * SIDE) & (lane < core * SIDE + SIDE), both, 0.0)
    lists, place, count = block_list(both, core * SIDE, SIDE, list_v.shape[1])
    over = jnp.broadcast_to(jnp.where(count > cap, 1.0, 0.0), (8, BLK))
    list_v[...] = lists.astype(jnp.int32)
    tab_v[...] = jnp.where((place < 0) | (place >= cap), float(cap), place).astype(jnp.int32)
    copies = [
        pltpu.make_async_copy(list_v, list_s, sem_loc.at[0]),
        pltpu.make_async_copy(tab_v, tab_s, sem_loc.at[1]),
    ]
    for copy in copies:
        copy.start()

    cell_log = log2(
        jnp.concatenate(
            [
                jnp.where(first, side_out[0], side_in[0]),
                jnp.where(first, side_in[0], side_out[0]),
            ],
            axis=0,
        )
    )
    spot_log = log2(smass[pl.ds(pl.multiple_of(core * SIDE, SIDE), SIDE), :])

    if not quick:
        lane_spread(-spot_norm, spread)
    wait_for(swap_in, sem_swap.at[3])

    def other_cells(i, _):
        for k in range(4):
            b = i * 4 + k
            wide = swap_in[b]
            chh[(1 - core) * 8 + b] = wide.astype(BF16)
            cells_turned((1 - core) * 8 + b, wide)
            if quick:
                cells_turned(core * 8 + b, swap_out[b])
        return 0

    lax.fori_loop(0, 2, other_cells, 0)
    for copy in copies:
        copy.wait()

    step = 26 if quick else 8

    def build(with_cross, with_crosst):
        def some(i, _):
            for k in range(step):
                e = i * step + k
                r = within(list_s[0, e], SIDE - 1)
                c = within(list_s[1, e], SIDE - 1)
                if with_cross:
                    cross[e] = jnp.dot(cht[r], shh[mid + c], preferred_element_type=F32) * CROSS
                if with_crosst:
                    crosst[e] = jnp.dot(sht[mid + c, :, :FEAT], chh[r], preferred_element_type=F32) * CROSS
            return 0

        lax.fori_loop(0, cap // step, some, 0)

    build(True, not quick)

    rows = lax.broadcasted_iota(jnp.int32, (SIDE, BLK), 0)

    def half(scores, other, own, feats):
        def body(i, carry):
            peak, total = carry
            parts = []
            for k in range(step):
                e = i * step + k
                o = within(list_s[other, e], SIDE - 1)
                v = scores[e] + spread[o]
                top = jnp.max(v, axis=0, keepdims=True)
                p = jnp.exp2(v - top)
                parts.append((list_s[own + 2, e], top, jnp.sum(p, axis=0, keepdims=True)))
                if feats is not None:
                    slot_peak[e] = top
                    blockmap[e] = jnp.dot(
                        feats(o), p.astype(BF16), preferred_element_type=F32
                    )
            for at, top, part in parts:
                new = jnp.where(rows == at, jnp.maximum(peak, top), peak)
                total = total * jnp.exp2(peak - new) + jnp.where(
                    rows == at, part * jnp.exp2(top - new), 0.0
                )
                peak = new
            return peak, total

        init = (jnp.full((SIDE, BLK), NEG, F32), jnp.zeros((SIDE, BLK), F32))
        return lax.fori_loop(0, cap // step, body, init)

    def joined(peak, total):
        return jnp.where(total > 0, peak + log2(jnp.maximum(total, 1e-30)), NEG)

    def merge(parts):
        top = parts[0]
        for part in parts[1:]:
            top = jnp.maximum(top, part)
        total = jnp.exp2(parts[0] - top)
        for part in parts[1:]:
            total = total + jnp.exp2(part - top)
        return top, total

    def settled(merged):
        return merged[0] + log2(merged[1])

    def cell_send(it, value):
        buf_e[it, eme] = value
        for _, dev, _, _ in e_peers:
            send(buf_e.at[it, eme], buf_e.at[it, eme], sem_e.at[0, it], sem_e.at[1, it], dev)

    def cell_merge(it):
        wait_for(buf_e.at[it, pl.ds(0, 15)], sem_e.at[1, it])
        return merge([buf_e[it, k] for k in range(16)])

    def spot_send(it, value):
        buf_d[it, dme] = value
        for _, dev, _ in d_peers:
            send(buf_d.at[it, dme], buf_d.at[it, dme], sem_d.at[0, it], sem_d.at[1, it], dev)

    def spot_merge(it):
        wait_for(buf_d.at[it, pl.ds(0, 7)], sem_d.at[1, it])
        return merge([buf_d[it, k] for k in range(8)])

    def peaks(i, carry):
        top_c, top_s = carry
        for k in range(step):
            e = i * step + k
            one = jnp.max(crosst[e], axis=0, keepdims=True)
            two = jnp.max(cross[e], axis=0, keepdims=True)
            top_c = jnp.where(rows == list_s[2, e], jnp.maximum(top_c, one), top_c)
            top_s = jnp.where(rows == list_s[3, e], jnp.maximum(top_s, two), top_s)
        return top_c, top_s

    def weights(i, _):
        for k in range(step):
            e = i * step + k
            r = within(list_s[0, e], SIDE - 1)
            c = within(list_s[1, e], SIDE - 1)
            weight_c[e] = jnp.exp2(crosst[e] - bound_c[pl.ds(r, 1), :])
            weight_s[e] = jnp.exp2(cross[e] - bound_s[pl.ds(c, 1), :])
        return 0

    def largest(pot):
        return jnp.max(jnp.max(pot, axis=0, keepdims=True), axis=1, keepdims=True)

    def quick_half(weight, bound, log_mass, merged, shift, other, own):
        lane_spread(jnp.exp2(log_mass - merged[0] - shift) / merged[1], spread)

        def body(i, total):
            parts = []
            for k in range(step):
                e = i * step + k
                o = within(list_s[other, e], SIDE - 1)
                parts.append(
                    (list_s[own + 2, e], jnp.sum(weight[e] * spread[o], axis=0, keepdims=True))
                )
            for at, part in parts:
                total = total + jnp.where(rows == at, part, 0.0)
            return total

        total = lax.fori_loop(0, cap // step, body, jnp.zeros((SIDE, BLK), F32))
        top = bound[...] + shift
        return top, jnp.where(total > 0, top + log2(jnp.maximum(total, 1e-38)), NEG)

    def watch(top, lse):
        near = (top - lse <= GAP) & (lse - top <= 1.5 * GAP) | (top < 0.5 * NEG) & (lse > 0.5 * NEG)
        worst[...] = jnp.where(near, worst[...], 1.0)

    def first_steps():
        wait_for(buf_0.at[pl.ds(0, 15)], sem_e.at[1, 0])
        cells = jnp.concatenate(
            [settled(merge([buf_0[2 * k + c] for k in range(8)])) for c in range(2)], axis=0
        )
        cells = cell_log - cells
        lane_spread(cells, spread)
        peak, total = half(cross, 0, 1, None)
        spot_send(0, joined(peak, total))
        build(False, True)
        init = jnp.full((SIDE, BLK), NEG, F32)
        top_c, top_s = lax.fori_loop(0, cap // step, peaks, (init, init))
        bound_c[...] = top_c
        bound_s[...] = top_s
        worst[...] = jnp.zeros((SIDE, BLK), F32)
        lax.fori_loop(0, cap // step, weights, 0)
        spots = spot_merge(0)

        def iteration(it, carry):
            spots, shift_c, shift_s = carry
            top, value = quick_half(weight_c, bound_c, spot_log, spots, shift_s, 1, 0)
            cell_send(it, value)
            cells = cell_merge(it)
            top_s, value = quick_half(weight_s, bound_s, cell_log, cells, shift_c, 0, 1)
            spot_send(it, value)
            lse = settled(cells)
            watch(top, lse)
            shift_c = largest(cell_log - lse)
            spots = spot_merge(it)
            lse = settled(spots)
            watch(top_s, lse)
            return spots, shift_c, largest(spot_log - lse)

        carry = (spots, largest(cells), largest(spot_log - settled(spots)))
        spots, _, _ = lax.fori_loop(1, ITERS - 1, iteration, carry)
        lane_spread(spot_log - settled(spots), spread)
        return jnp.maximum(over_0, jnp.max(worst[...], axis=0, keepdims=True))

    def first_steps_whole():
        def iteration(it, _):
            peak, total = half(crosst, 1, 0, None)
            cell_send(it, joined(peak, total))
            lane_spread(cell_log - settled(cell_merge(it)), spread)
            peak, total = half(cross, 0, 1, None)
            spot_send(it, joined(peak, total))
            lane_spread(spot_log - settled(spot_merge(it)), spread)
            return 0

        lax.fori_loop(0, ITERS - 1, iteration, 0)
        return jnp.zeros((1, BLK), F32)

    over = jnp.maximum(over, first_steps() if quick else first_steps_whole())

    def gather_maps(peak, total, msg, transposed):
        peak_scr[...] = peak
        blockmap[cap] = jnp.zeros((FEAT, BLK), F32)
        slot_peak[cap] = jnp.full((1, BLK), NEG, F32)

        def one(b, _):
            top = peak_scr[pl.ds(b, 1), :]
            acc = jnp.zeros((FEAT, BLK), F32)
            for k in range(SIDE):
                e = tab_s[k, core * SIDE + b] if transposed else tab_s[b, core * SIDE + k]
                e = within(e, cap)
                acc = acc + blockmap[e] * jnp.exp2(slot_peak[e] - top)
            msg[b, pl.ds(0, FEAT), :] = acc
            return 0

        lax.fori_loop(0, SIDE, one, 0)
        for b in range(SIDE):
            msg[b, pl.ds(FEAT, 8), :] = jnp.concatenate(
                [peak[b : b + 1], total[b : b + 1], jnp.zeros((6, BLK), F32)], axis=0
            )

    def total_map(take, n):
        top = take(0, pl.ds(FEAT, 8))[0:1]
        for k in range(1, n):
            top = jnp.maximum(top, take(k, pl.ds(FEAT, 8))[0:1])
        total = jnp.zeros((1, BLK), F32)
        acc = jnp.zeros((FEAT, BLK), F32)
        for k in range(n):
            stat = take(k, pl.ds(FEAT, 8))
            scale = jnp.exp2(stat[0:1] - top)
            total = total + stat[1:2] * scale
            acc = acc + take(k, pl.ds(0, FEAT)) * scale
        return top + log2(total), acc / total

    peak, total = half(crosst, 1, 0, lambda o: shh[mid + o])
    cell_send(ITERS - 1, joined(peak, total))
    flag_e[eme] = over
    for _, dev, _, _ in e_peers:
        send(flag_e.at[eme], flag_e.at[eme], sem_e.at[0, ITERS], sem_e.at[1, ITERS], dev)
    gather_maps(peak, total, msg_c, False)
    for _, dev, s2, k2 in e_peers:
        send(msg_c.at[k2 * 8 + s2], rcv_c.at[eme], sem_map.at[0], sem_map.at[1], dev)
    rcv_c[eme] = msg_c[core * 8 + si]
    cell_pot = cell_log - settled(cell_merge(ITERS - 1))
    lane_spread(cell_pot, spread)

    peak, total = half(cross, 0, 1, lambda o: chh[o])
    gather_maps(peak, total, msg_s, True)
    for _, dev, d2 in d_peers:
        send(msg_s.at[pl.ds(d2 * 2, 2)], rcv_s.at[dme], sem_map.at[2], sem_map.at[3], dev)
    rcv_s[dme] = msg_s[pl.ds(dme * 2, 2)]

    wait_for(flag_e.at[pl.ds(0, 15)], sem_e.at[1, ITERS])
    over = flag_e[0]
    for k in range(1, 16):
        over = jnp.maximum(over, flag_e[k])
    flag_d[dme] = over
    for _, dev, _ in d_peers:
        send(flag_d.at[dme], flag_d.at[dme], sem_d.at[0, ITERS], sem_d.at[1, ITERS], dev)

    wait_for(rcv_c.at[pl.ds(0, 15)], sem_map.at[1])
    _, block = total_map(lambda k, r: rcv_c[k, r, :], 16)
    own_c[...] = block
    at = pl.ds(pl.multiple_of(si * BLK, BLK), BLK)
    cmap_out[:, at] = block
    for a in range(2):
        for b in (2, 1, 3, 0):
            if a or b:
                s2 = lax.rem(yhi + a, 2) * 4 + lax.rem(zz + b, 4)
                send(own_c, cmap_out.at[:, at], sem_map.at[4], sem_map.at[5], (ci, s2))

    wait_for(rcv_s.at[pl.ds(0, 7)], sem_map.at[3])
    lses = []
    for h in range(2):
        lse, block = total_map(lambda k, r: rcv_s[k, h, r, :], 8)
        own_s[:, pl.ds(h * BLK, BLK)] = block
        lses.append(lse)
    pot_s[dme] = jnp.concatenate(lses + [jnp.zeros((6, BLK), F32)], axis=0)
    half_at = core * SIDE * BLK
    at = pl.ds(pl.multiple_of(half_at + dme * 2 * BLK, 2 * BLK), 2 * BLK)
    smap_out[:, at] = own_s[...]
    for _, dev, _ in d_peers:
        send(pot_s.at[dme], pot_s.at[dme], sem_map.at[6], sem_map.at[7], dev)
        send(own_s, smap_out.at[:, at], sem_map.at[8], sem_map.at[9], dev)

    cell_norm = jnp.zeros((8, BLK), F32)
    rows8 = lax.broadcasted_iota(jnp.int32, (8, BLK), 0)
    for b in range(8):
        wide = swap_out[b]
        cell_norm = jnp.where(
            rows8 == b, jnp.sum(wide * wide, axis=0, keepdims=True) * NORM, cell_norm
        )
    cell_own = jnp.where(first, cell_pot[0:8], cell_pot[8:16])
    cpot_out[...] = (cell_own + cell_norm) * (1.0 / UNIT)

    wait_for(pot_s.at[pl.ds(0, 7)], sem_map.at[7])
    lse = jnp.concatenate([pot_s[k, 0:2, :] for k in range(8)], axis=0)
    half_rows = pl.ds(pl.multiple_of(core * SIDE, SIDE), SIDE)
    spot_out[half_rows, :] = (spot_log - lse + spot_norm) * (1.0 / UNIT)
    send(spot_out.at[half_rows], spot_out.at[half_rows], sem_swap.at[4], sem_swap.at[5], partner)
    half_cols = pl.ds(pl.multiple_of(half_at, SIDE * BLK), SIDE * BLK)
    part = smap_out.at[:, pl.ds(0, 7 * 2 * BLK)]
    wait_for(part, sem_map.at[9])
    send(smap_out.at[:, half_cols], smap_out.at[:, half_cols], sem_swap.at[6], sem_swap.at[7], partner)

    wait_for(flag_d.at[pl.ds(0, 7)], sem_d.at[1, ITERS])
    over = flag_d[0]
    for k in range(1, 8):
        over = jnp.maximum(over, flag_d[k])
    flag_out[0] = jnp.max(over).astype(jnp.int32)

    wait_for(cmap_out.at[:, pl.ds(0, 7 * BLK)], sem_map.at[5])
    wait_for(spot_out.at[pl.ds(0, SIDE)], sem_swap.at[5])
    wait_for(smap_out.at[:, pl.ds(0, SIDE * BLK)], sem_swap.at[7])
    wait_for(side_out, sem_swap.at[0])
    wait_for(swap_out, sem_swap.at[2])
    wait_for(spot_out.at[pl.ds(0, SIDE)], sem_swap.at[4])
    wait_for(smap_out.at[:, pl.ds(0, SIDE * BLK)], sem_swap.at[6])
    wait_for(rcv_c.at[pl.ds(0, 15)], sem_map.at[0])
    wait_for(rcv_s.at[pl.ds(0, 7)], sem_map.at[2])
    wait_for(cmap_out.at[:, pl.ds(0, 7 * BLK)], sem_map.at[4])
    wait_for(pot_s.at[pl.ds(0, 7)], sem_map.at[6])
    wait_for(part, sem_map.at[8])
    wait_for(flag_e.at[pl.ds(0, 15)], sem_e.at[0, ITERS])
    wait_for(flag_d.at[pl.ds(0, 7)], sem_d.at[0, ITERS])

    def sent(it, _):
        wait_for(buf_e.at[it, pl.ds(0, 15)], sem_e.at[0, it])
        wait_for(buf_d.at[it, pl.ds(0, 7)], sem_d.at[0, it])
        return 0

    if quick:
        wait_for(buf_0.at[pl.ds(0, 15)], sem_e.at[0, 0])
        wait_for(buf_d.at[0, pl.ds(0, 7)], sem_d.at[0, 0])
    lax.fori_loop(1 if quick else 0, ITERS - 1, sent, 0)
    wait_for(buf_e.at[ITERS - 1, pl.ds(0, 15)], sem_e.at[0, ITERS - 1])


def run(cap, quick, collective, cfeat, sfeat, cmass, smass, pattern):
    width = 128 if cap <= 128 else 256
    spots = 2 * SIDE if quick else SIDE
    vmem = lambda *shape: pltpu.VMEM(shape, F32)
    half = lambda *shape: pltpu.VMEM(shape, BF16)
    shape = lambda *dims: jax.ShapeDtypeStruct(dims, F32)
    scratch = [
        half(FEAT, 1024), half(FEAT, 4096), vmem(8, BLK), vmem(32, BLK), pltpu.VMEM((8, 32), jnp.int32),
        vmem(8, FEAT, BLK), vmem(8, FEAT, BLK), vmem(2, 8, BLK), vmem(2, 8, BLK),
        half(SIDE, FEAT, BLK), half(SIDE, BLK, FEAT), half(spots, FEAT, BLK), half(spots, BLK, DEEP if quick else FEAT),
        vmem(cap, BLK, BLK), vmem(cap, BLK, BLK), vmem(SIDE, BLK, BLK),
        vmem(cap + 1, FEAT, BLK), vmem(cap + 1, 1, BLK), vmem(SIDE, BLK),
        pltpu.VMEM((8, width), jnp.int32), pltpu.SMEM((8, width), jnp.int32),
        pltpu.VMEM((SIDE, BLK), jnp.int32), pltpu.SMEM((SIDE, BLK), jnp.int32),
        vmem(ITERS, 16, SIDE, BLK), vmem(ITERS - 1, 8, SIDE, BLK), vmem(16, 8, BLK), vmem(8, 8, BLK),
        vmem(SIDE, MSG, BLK), vmem(16, MSG, BLK), vmem(SIDE, MSG, BLK), vmem(8, 2, MSG, BLK),
        vmem(FEAT, BLK), vmem(FEAT, 2 * BLK), vmem(8, 8, BLK),
        pltpu.SemaphoreType.DMA((8,)), pltpu.SemaphoreType.DMA((2, ITERS + 1)),
        pltpu.SemaphoreType.DMA((2, ITERS + 1)), pltpu.SemaphoreType.DMA((10,)),
        pltpu.SemaphoreType.DMA((3,)), pltpu.SemaphoreType.DMA((5,)),
    ]
    if quick:
        scratch += [
            vmem(cap, BLK, BLK), vmem(cap, BLK, BLK), vmem(SIDE, BLK), vmem(SIDE, BLK), vmem(SIDE, BLK),
            half(8, DEEP, BLK), pltpu.VMEM((8, BLK), jnp.int32), pltpu.SMEM((8, BLK), jnp.int32),
            vmem(16, 8, BLK),
        ]
    return pl.pallas_call(
        functools.partial(sinkhorn_kernel, cap, quick),
        out_shape=(shape(8, BLK), shape(32, BLK), shape(FEAT, 1024), shape(FEAT, 4096), jax.ShapeDtypeStruct((1,), jnp.int32)),
        in_specs=[pl.BlockSpec(memory_space=pltpu.HBM)] * 5,
        out_specs=tuple([pl.BlockSpec(memory_space=pltpu.VMEM)] * 4 + [pl.BlockSpec(memory_space=pltpu.SMEM)]),
        scratch_shapes=scratch,
        compiler_params=pltpu.CompilerParams(
            collective_id=collective, has_side_effects=True, vmem_limit_bytes=60 * 2**20
        ),
    )(cfeat, sfeat, cmass, smass, pattern)


def place_kernel(*refs):
    srcs, dsts, sems = refs[:4], refs[4:8], refs[8]
    copies = [pltpu.make_async_copy(s, d, sems.at[k]) for k, (s, d) in enumerate(zip(srcs, dsts))]
    for copy in copies:
        copy.start()
    for copy in copies:
        copy.wait()


def place(*arrays):
    return pl.pallas_call(
        place_kernel,
        out_shape=tuple(jax.ShapeDtypeStruct(a.shape, a.dtype) for a in arrays),
        in_specs=[pl.BlockSpec(memory_space=pl.ANY)] * 4,
        out_specs=tuple([pl.BlockSpec(memory_space=pl.ANY)] * 4),
        scratch_shapes=[pltpu.SemaphoreType.DMA((4,))],
    )(*arrays)


def per_device(cell_feat, spot_feat, cell_mass, spot_mass, block_pattern):
    args = (cell_feat.T, spot_feat.T, cell_mass.reshape(8, BLK), spot_mass.reshape(32, BLK), block_pattern)
    outs = run(52, True, 0, *args)
    cpot, spot, cmap, smap = lax.cond(
        outs[4][0] > 0, lambda now: place(*run(SIDE * SIDE, False, 1, *args)[:4]), lambda now: place(*now[:4]), outs
    )
    return cpot.reshape(1024), spot.reshape(4096), cmap.T, smap.T


def solution(mesh):
    in_specs = (P("cells", None), P("spots", None), P("cells"), P("spots"), P("cells", "spots"))
    out_specs = (P("cells"), P("spots"), P("cells", None), P("spots", None))
    return jax.shard_map(
        per_device, mesh=mesh, in_specs=in_specs, out_specs=out_specs, check_vma=False
    )
```

```python
import functools
import math

import jax
import jax.numpy as jnp
from jax import lax
from jax.experimental import pallas as pl
from jax.experimental.pallas import tpu as pltpu
from jax.sharding import PartitionSpec as P

FEAT = 64
BLK = 128
ITERS = 5
EPSILON = 0.05
NEG = -1e30
LOG2E = math.log2(math.e)
UNIT = LOG2E / EPSILON
CROSS = UNIT * 2.0 / FEAT
NORM = UNIT / FEAT
SIDE = 16
FIRST = 56
GAP = 90.0
DEEP = FEAT + 16
MSG = FEAT + 8
MESH = pl.DeviceIdType.MESH
F32 = jnp.float32
BF16 = jnp.bfloat16


def log2(v):
    return jnp.log(v) * LOG2E


def wait_for(view, sem):
    pltpu.make_async_copy(view, view, sem).wait()


def send(src, dst, ssem, rsem, dev):
    pltpu.make_async_remote_copy(
        src_ref=src, dst_ref=dst, send_sem=ssem, recv_sem=rsem, device_id=dev, device_id_type=MESH
    ).start()


def within(index, top):
    return jnp.minimum(jnp.maximum(index, 0), top)


def ring(offset):
    return {0: 0, 1: 1, 2: 2, 3: 1}[offset]


def lane_spread(pot, out):
    for b in range(SIDE):
        out[b] = jnp.transpose(jnp.broadcast_to(pot[b : b + 1], (BLK, BLK)))


def block_list(allowed, lane0, cols, width):
    rows = allowed.shape[0]
    upto = (
        lax.broadcasted_iota(jnp.int32, (BLK, BLK), 0)
        < lax.broadcasted_iota(jnp.int32, (BLK, BLK), 1)
    ).astype(BF16)
    inside = jnp.dot(allowed.astype(BF16), upto, preferred_element_type=F32)
    per_row = jnp.broadcast_to(jnp.sum(allowed, axis=1, keepdims=True), (rows, BLK))
    below = lax.broadcasted_iota(jnp.int32, (rows, BLK), 0)
    before = jnp.zeros((rows, BLK), F32)
    for r in range(rows - 1):
        before = before + jnp.where(below > r, per_row[r : r + 1], 0.0)
    place = jnp.where(allowed > 0, before + inside, -1.0)
    count = jnp.sum(jnp.sum(allowed, axis=1, keepdims=True), axis=0, keepdims=True)
    pairs = rows * cols
    wide_place = jnp.broadcast_to(place[:, None, :], (rows, cols, BLK)).reshape(pairs, BLK)
    pair = lax.broadcasted_iota(jnp.int32, (pairs, BLK), 0)
    pair_lane = lax.broadcasted_iota(jnp.int32, (pairs, BLK), 1)
    chosen = pair_lane == lane0 + pair % cols
    slot_of = jnp.sum(jnp.where(chosen, wide_place, 0.0), axis=1, keepdims=True)
    hot = slot_of == lax.broadcasted_iota(jnp.int32, (pairs, width), 1).astype(F32)
    kind = lax.broadcasted_iota(jnp.int32, (8, pairs), 0)
    which = lax.broadcasted_iota(jnp.int32, (8, pairs), 1)
    facts = jnp.where(kind == 0, which // cols, jnp.where(kind == 1, which % cols, 1))
    lists = jnp.dot(
        facts.astype(F32).astype(BF16), hot.astype(F32).astype(BF16), preferred_element_type=F32
    )
    none = 99.0 * (1.0 - lists[2:3])
    kind = lax.broadcasted_iota(jnp.int32, (8, width), 0)
    lists = jnp.where(kind >= 2, 0.0, lists) + jnp.where(
        kind == 2, lists[0:1] + none, jnp.where(kind == 3, lists[1:2] + none, 0.0)
    )
    return lists, place, count


def sinkhorn_kernel(
    cap, quick, cfeat_h, sfeat_h, cmass_h, smass_h, pattern_h,
    cpot_out, spot_out, cmap_out, smap_out, flag_out,
    cfeat, sfeat, cmass, smass, pattern, swap_out, swap_in, side_out, side_in, chh, cht, shh, sht, cross, crosst, spread,
    blockmap, slot_peak, peak_scr, list_v, list_s, tab_v, tab_s,
    buf_e, buf_d, flag_e, flag_d, msg_c, rcv_c, msg_s, rcv_s, own_c, own_s, pot_s,
    sem_swap, sem_e, sem_d, sem_map, sem_loc, sem_in, sem_ag, *more,
):
    ci = lax.axis_index("cells")
    si = lax.axis_index("spots")
    core = ci % 2
    dme = ci // 2
    ylo, xx = dme // 4, dme % 4
    yhi, zz = si // 4, si % 4
    eme = si * 2 + core
    partner = (ci + 1 - 2 * core, si)

    e_peers = []
    for a in range(2):
        for b in range(4):
            for k in range(2):
                if a or b or k:
                    s2 = lax.rem(yhi + a, 2) * 4 + lax.rem(zz + b, 4)
                    k2 = lax.rem(core + k, 2)
                    e_peers.append((2 * a + ring(b) + 0.1 * k, (dme * 2 + k2, s2), s2, k2))
    e_peers.sort(key=lambda item: -item[0])
    d_peers = []
    for a in range(2):
        for b in range(4):
            if a or b:
                d2 = lax.rem(ylo + a, 2) * 4 + lax.rem(xx + b, 4)
                d_peers.append((a + ring(b), (d2 * 2 + core, si), d2))
    d_peers.sort(key=lambda item: -item[0])

    if quick:
        weight_c, weight_s, bound_c, bound_s, worst, chx, list0_v, list0_s, buf_0 = more

    barrier = pltpu.get_barrier_semaphore()
    for item in e_peers + d_peers:
        pl.semaphore_signal(barrier, inc=1, device_id=item[1], device_id_type=MESH)

    loads = [
        pltpu.make_async_copy(src, dst, sem_in.at[k])
        for k, (src, dst) in enumerate(
            ((pattern_h, pattern), (cfeat_h, cfeat), (sfeat_h, sfeat), (cmass_h, cmass), (smass_h, smass))
        )
    ]
    for load in loads:
        load.start()
    loads[0].wait()
    pattern_own = (pattern[...] > 0).astype(F32)
    side_out[1] = jnp.concatenate([pattern_own, jnp.zeros((8, BLK - 32), F32)], axis=1)
    if quick:
        lists, _, count_0 = block_list(side_out[1], 0, 2 * SIDE, list0_v.shape[1])
        list0_v[...] = lists.astype(jnp.int32)
        copy_0 = pltpu.make_async_copy(list0_v, list0_s, sem_loc.at[2])
        copy_0.start()
    loads[1].wait()
    below = lax.broadcasted_iota(jnp.int32, (DEEP - FEAT, BLK), 0)

    def cells_turned(b, wide):
        cht[b] = jnp.transpose(wide).astype(BF16)

    def own_cells(i, _):
        for k in range(4):
            b = i * 4 + k
            block = cfeat[:, pl.ds(pl.multiple_of(b * BLK, BLK), BLK)]
            wide = block.astype(F32)
            swap_out[b] = wide
            chh[core * 8 + b] = block
            if quick:
                ones = jnp.where(below < 3, 1.0, 0.0).astype(BF16)
                chx[b] = jnp.concatenate([block, ones], axis=0)
            else:
                cells_turned(core * 8 + b, wide)
        return 0

    lax.fori_loop(0, 2, own_cells, 0)
    loads[2].wait()

    spots = 2 * SIDE if quick else SIDE
    offset = 0 if quick else core * SIDE
    mid = core * SIDE if quick else 0

    def own_spots(i, norms):
        for k in range(4):
            b = i * 4 + k
            block = sfeat[:, pl.ds(pl.multiple_of((offset + b) * BLK, BLK), BLK)]
            wide = block.astype(F32)
            norm = jnp.sum(wide * wide, axis=0, keepdims=True)
            shh[b] = block
            if quick:
                rest = norm * -0.5
                parts = jnp.zeros((DEEP - FEAT, BLK), F32)
                for n in range(3):
                    part = rest.astype(BF16).astype(F32)
                    parts = jnp.where(below == n, part, parts)
                    rest = rest - part
                wide = jnp.concatenate([wide, parts], axis=0)
            sht[b] = jnp.transpose(wide).astype(BF16)
            here = lax.broadcasted_iota(jnp.int32, (SIDE, BLK), 0) == b - mid
            norms = jnp.where(here, norm * NORM, norms)
        return norms

    spot_norm = lax.fori_loop(0, spots // 4, own_spots, jnp.zeros((SIDE, BLK), F32))

    def first_half():
        copy_0.wait()
        rows8 = lax.broadcasted_iota(jnp.int32, (8, BLK), 0)
        step = 14

        def body(i, carry):
            peak, total = carry
            parts = []
            for k in range(step):
                e = i * step + k
                r = within(list0_s[0, e], 7)
                c = within(list0_s[1, e], 2 * SIDE - 1)
                v = jnp.dot(sht[c], chx[r], preferred_element_type=F32) * CROSS
                top = jnp.max(v, axis=0, keepdims=True)
                part = jnp.sum(jnp.exp2(v - top), axis=0, keepdims=True)
                parts.append((list0_s[2, e], top, part))
            for at, top, part in parts:
                new = jnp.where(rows8 == at, jnp.maximum(peak, top), peak)
                total = total * jnp.exp2(peak - new) + jnp.where(
                    rows8 == at, part * jnp.exp2(top - new), 0.0
                )
                peak = new
            return peak, total

        init = (jnp.full((8, BLK), NEG, F32), jnp.zeros((8, BLK), F32))
        peak, total = lax.fori_loop(0, FIRST // step, body, init)
        buf_0[eme] = jnp.where(total > 0, peak + log2(jnp.maximum(total, 1e-30)), NEG)
        return jnp.where(count_0 > FIRST, 1.0, 0.0)

    over_0 = first_half() if quick else None
    pl.semaphore_wait(barrier, len(e_peers) + len(d_peers))
    loads[3].wait()
    loads[4].wait()
    side_out[0] = cmass[...]
    if quick:
        for _, dev, _, _ in e_peers:
            send(buf_0.at[eme], buf_0.at[eme], sem_e.at[0, 0], sem_e.at[1, 0], dev)

    send(side_out, side_in, sem_swap.at[0], sem_swap.at[1], partner)
    send(swap_out, swap_in, sem_swap.at[2], sem_swap.at[3], partner)
    wait_for(side_in, sem_swap.at[1])

    first = core == 0
    mine, theirs = side_out[1], side_in[1]
    lane = lax.broadcasted_iota(jnp.int32, (SIDE, BLK), 1)
    both = jnp.concatenate(
        [jnp.where(first, mine, theirs), jnp.where(first, theirs, mine)], axis=0
    )
    both = jnp.where((lane >= core * SIDE) & (lane < core * SIDE + SIDE), both, 0.0)
    lists, place, count = block_list(both, core * SIDE, SIDE, list_v.shape[1])
    over = jnp.broadcast_to(jnp.where(count > cap, 1.0, 0.0), (8, BLK))
    list_v[...] = lists.astype(jnp.int32)
    tab_v[...] = jnp.where((place < 0) | (place >= cap), float(cap), place).astype(jnp.int32)
    copies = [
        pltpu.make_async_copy(list_v, list_s, sem_loc.at[0]),
        pltpu.make_async_copy(tab_v, tab_s, sem_loc.at[1]),
    ]
    for copy in copies:
        copy.start()

    cell_log = log2(
        jnp.concatenate(
            [
                jnp.where(first, side_out[0], side_in[0]),
                jnp.where(first, side_in[0], side_out[0]),
            ],
            axis=0,
        )
    )
    spot_log = log2(smass[pl.ds(pl.multiple_of(core * SIDE, SIDE), SIDE), :])

    if not quick:
        lane_spread(-spot_norm, spread)
    wait_for(swap_in, sem_swap.at[3])

    def other_cells(i, _):
        for k in range(4):
            b = i * 4 + k
            wide = swap_in[b]
            chh[(1 - core) * 8 + b] = wide.astype(BF16)
            cells_turned((1 - core) * 8 + b, wide)
            if quick:
                cells_turned(core * 8 + b, swap_out[b])
        return 0

    lax.fori_loop(0, 2, other_cells, 0)
    for copy in copies:
        copy.wait()

    step = 26 if quick else 8

    def build(with_cross, with_crosst):
        def some(i, _):
            for k in range(step):
                e = i * step + k
                r = within(list_s[0, e], SIDE - 1)
                c = within(list_s[1, e], SIDE - 1)
                if with_cross:
                    cross[e] = jnp.dot(cht[r], shh[mid + c], preferred_element_type=F32) * CROSS
                if with_crosst:
                    crosst[e] = jnp.dot(sht[mid + c, :, :FEAT], chh[r], preferred_element_type=F32) * CROSS
            return 0

        lax.fori_loop(0, cap // step, some, 0)

    build(True, not quick)

    rows = lax.broadcasted_iota(jnp.int32, (SIDE, BLK), 0)

    def half(scores, other, own, feats):
        def body(i, carry):
            peak, total = carry
            parts = []
            for k in range(step):
                e = i * step + k
                o = within(list_s[other, e], SIDE - 1)
                v = scores[e] + spread[o]
                top = jnp.max(v, axis=0, keepdims=True)
                p = jnp.exp2(v - top)
                parts.append((list_s[own + 2, e], top, jnp.sum(p, axis=0, keepdims=True)))
                if feats is not None:
                    slot_peak[e] = top
                    blockmap[e] = jnp.dot(
                        feats(o), p.astype(BF16), preferred_element_type=F32
                    )
            for at, top, part in parts:
                new = jnp.where(rows == at, jnp.maximum(peak, top), peak)
                total = total * jnp.exp2(peak - new) + jnp.where(
                    rows == at, part * jnp.exp2(top - new), 0.0
                )
                peak = new
            return peak, total

        init = (jnp.full((SIDE, BLK), NEG, F32), jnp.zeros((SIDE, BLK), F32))
        return lax.fori_loop(0, cap // step, body, init)

    def joined(peak, total):
        return jnp.where(total > 0, peak + log2(jnp.maximum(total, 1e-30)), NEG)

    def merge(parts):
        top = parts[0]
        for part in parts[1:]:
            top = jnp.maximum(top, part)
        total = jnp.exp2(parts[0] - top)
        for part in parts[1:]:
            total = total + jnp.exp2(part - top)
        return top, total

    def settled(merged):
        return merged[0] + log2(merged[1])

    def cell_send(it, value):
        buf_e[it, eme] = value
        for _, dev, _, _ in e_peers:
            send(buf_e.at[it, eme], buf_e.at[it, eme], sem_e.at[0, it], sem_e.at[1, it], dev)

    def cell_merge(it):
        wait_for(buf_e.at[it, pl.ds(0, 15)], sem_e.at[1, it])
        return merge([buf_e[it, k] for k in range(16)])

    def spot_send(it, value):
        buf_d[it, dme] = value
        for _, dev, _ in d_peers:
            send(buf_d.at[it, dme], buf_d.at[it, dme], sem_d.at[0, it], sem_d.at[1, it], dev)

    def spot_merge(it):
        wait_for(buf_d.at[it, pl.ds(0, 7)], sem_d.at[1, it])
        return merge([buf_d[it, k] for k in range(8)])

    def peaks(i, carry):
        top_c, top_s = carry
        for k in range(step):
            e = i * step + k
            one = jnp.max(crosst[e], axis=0, keepdims=True)
            two = jnp.max(cross[e], axis=0, keepdims=True)
            top_c = jnp.where(rows == list_s[2, e], jnp.maximum(top_c, one), top_c)
            top_s = jnp.where(rows == list_s[3, e], jnp.maximum(top_s, two), top_s)
        return top_c, top_s

    def weights(i, _):
        for k in range(step):
            e = i * step + k
            r = within(list_s[0, e], SIDE - 1)
            c = within(list_s[1, e], SIDE - 1)
            weight_c[e] = jnp.exp2(crosst[e] - bound_c[pl.ds(r, 1), :])
            weight_s[e] = jnp.exp2(cross[e] - bound_s[pl.ds(c, 1), :])
        return 0

    def largest(pot):
        return jnp.max(jnp.max(pot, axis=0, keepdims=True), axis=1, keepdims=True)

    def quick_half(weight, bound, log_mass, merged, shift, other, own):
        lane_spread(jnp.exp2(log_mass - merged[0] - shift) / merged[1], spread)

        def body(i, total):
            parts = []
            for k in range(step):
                e = i * step + k
                o = within(list_s[other, e], SIDE - 1)
                parts.append(
                    (list_s[own + 2, e], jnp.sum(weight[e] * spread[o], axis=0, keepdims=True))
                )
            for at, part in parts:
                total = total + jnp.where(rows == at, part, 0.0)
            return total

        total = lax.fori_loop(0, cap // step, body, jnp.zeros((SIDE, BLK), F32))
        top = bound[...] + shift
        return top, jnp.where(total > 0, top + log2(jnp.maximum(total, 1e-38)), NEG), total

    def watch(top, lse):
        near = (top - lse <= GAP) & (lse - top <= 1.5 * GAP) | (top < 0.5 * NEG) & (lse > 0.5 * NEG)
        worst[...] = jnp.where(near, worst[...], 1.0)

    def first_steps():
        wait_for(buf_0.at[pl.ds(0, 15)], sem_e.at[1, 0])
        cells = jnp.concatenate(
            [settled(merge([buf_0[2 * k + c] for k in range(8)])) for c in range(2)], axis=0
        )
        cells = cell_log - cells
        lane_spread(cells, spread)
        peak, total = half(cross, 0, 1, None)
        spot_send(0, joined(peak, total))
        build(False, True)
        init = jnp.full((SIDE, BLK), NEG, F32)
        top_c, top_s = lax.fori_loop(0, cap // step, peaks, (init, init))
        bound_c[...] = top_c
        bound_s[...] = top_s
        worst[...] = jnp.zeros((SIDE, BLK), F32)
        lax.fori_loop(0, cap // step, weights, 0)
        spots = spot_merge(0)

        def iteration(it, carry):
            spots, shift_c, shift_s = carry
            top, value, _ = quick_half(weight_c, bound_c, spot_log, spots, shift_s, 1, 0)
            cell_send(it, value)
            cells = cell_merge(it)
            top_s, value, _ = quick_half(weight_s, bound_s, cell_log, cells, shift_c, 0, 1)
            spot_send(it, value)
            lse = settled(cells)
            watch(top, lse)
            shift_c = largest(cell_log - lse)
            spots = spot_merge(it)
            lse = settled(spots)
            watch(top_s, lse)
            return spots, shift_c, largest(spot_log - lse)

        carry = (spots, largest(cells), largest(spot_log - settled(spots)))
        spots, _, shift_s = lax.fori_loop(1, ITERS - 1, iteration, carry)
        return over_0, (spots, shift_s)

    def first_steps_whole():
        def iteration(it, _):
            peak, total = half(crosst, 1, 0, None)
            cell_send(it, joined(peak, total))
            lane_spread(cell_log - settled(cell_merge(it)), spread)
            peak, total = half(cross, 0, 1, None)
            spot_send(it, joined(peak, total))
            lane_spread(spot_log - settled(spot_merge(it)), spread)
            return 0

        lax.fori_loop(0, ITERS - 1, iteration, 0)
        return jnp.zeros((1, BLK), F32), None

    more_over, last = first_steps() if quick else first_steps_whole()
    over = jnp.maximum(over, more_over)

    def gather_maps(peak, total, msg, transposed, order, send_pair, plain):
        peak_scr[0] = peak
        peak_scr[1] = total
        blockmap[cap] = jnp.zeros((FEAT, BLK), F32)
        slot_peak[cap] = jnp.full((1, BLK), NEG, F32)

        def one(b):
            top = peak_scr[0, pl.ds(b, 1), :]
            acc = jnp.zeros((FEAT, BLK), F32)
            for k in range(SIDE):
                e = tab_s[k, core * SIDE + b] if transposed else tab_s[b, core * SIDE + k]
                e = within(e, cap)
                acc = acc + (blockmap[e] if plain else blockmap[e] * jnp.exp2(slot_peak[e] - top))
            msg[b, pl.ds(0, FEAT), :] = acc
            msg[b, pl.ds(FEAT, 8), :] = jnp.concatenate(
                [top, peak_scr[1, pl.ds(b, 1), :], jnp.zeros((6, BLK), F32)], axis=0
            )

        if order is None:
            lax.fori_loop(0, SIDE, lambda b, _: (one(b), 0)[1], 0)
        else:
            for d2 in order:
                lax.fori_loop(0, 2, lambda h, _: (one(2 * d2 + h), 0)[1], 0)
                send_pair(d2)

    def total_map(take, n):
        top = take(0, pl.ds(FEAT, 8))[0:1]
        for k in range(1, n):
            top = jnp.maximum(top, take(k, pl.ds(FEAT, 8))[0:1])
        total = jnp.zeros((1, BLK), F32)
        acc = jnp.zeros((FEAT, BLK), F32)
        for k in range(n):
            stat = take(k, pl.ds(FEAT, 8))
            scale = jnp.exp2(stat[0:1] - top)
            total = total + stat[1:2] * scale
            acc = acc + take(k, pl.ds(0, FEAT)) * scale
        return top + log2(total), acc / total

    def send_flag():
        flag_e[eme] = jnp.maximum(over, jnp.max(worst[...], axis=0, keepdims=True)) if quick else over
        for _, dev, _, _ in e_peers:
            send(flag_e.at[eme], flag_e.at[eme], sem_e.at[0, ITERS], sem_e.at[1, ITERS], dev)

    if quick:
        last_top, value, total = quick_half(weight_c, bound_c, spot_log, last[0], last[1], 1, 0)
        cell_send(ITERS - 1, value)
        peak = last_top

        def quick_maps(i, _):
            for k in range(step):
                e = i * step + k
                o = within(list_s[1, e], SIDE - 1)
                blockmap[e] = jnp.dot(
                    shh[mid + o], (weight_c[e] * spread[o]).astype(BF16), preferred_element_type=F32
                )
            return 0

        lax.fori_loop(0, cap // step, quick_maps, 0)
    else:
        peak, total = half(crosst, 1, 0, lambda o: shh[mid + o])
        cell_send(ITERS - 1, joined(peak, total))
        send_flag()
    gather_maps(peak, total, msg_c, False, None, None, quick)
    for _, dev, s2, k2 in e_peers:
        send(msg_c.at[k2 * 8 + s2], rcv_c.at[eme], sem_map.at[0], sem_map.at[1], dev)
    rcv_c[eme] = msg_c[core * 8 + si]
    cell_lse = settled(cell_merge(ITERS - 1))
    cell_pot = cell_log - cell_lse
    lane_spread(cell_pot, spread)
    if quick:
        watch(last_top, cell_lse)

    peak, total = half(cross, 0, 1, lambda o: chh[o])
    def send_pair(d2):
        for _, dev, other in d_peers:
            if other is d2:
                send(msg_s.at[pl.ds(d2 * 2, 2)], rcv_s.at[dme], sem_map.at[2], sem_map.at[3], dev)

    gather_maps(peak, total, msg_s, True, [d2 for _, _, d2 in d_peers] + [dme], send_pair, False)
    rcv_s[dme] = msg_s[pl.ds(dme * 2, 2)]
    if quick:
        send_flag()

    wait_for(rcv_c.at[pl.ds(0, 15)], sem_map.at[1])
    _, block = total_map(lambda k, r: rcv_c[k, r, :], 16)
    own_c[...] = block
    at = pl.ds(pl.multiple_of(si * BLK, BLK), BLK)
    cmap_out[:, at] = block
    for a in range(2):
        for b in (2, 1, 3, 0):
            if a or b:
                s2 = lax.rem(yhi + a, 2) * 4 + lax.rem(zz + b, 4)
                send(own_c, cmap_out.at[:, at], sem_map.at[4], sem_map.at[5], (ci, s2))

    wait_for(rcv_s.at[pl.ds(0, 7)], sem_map.at[3])
    lses = []
    for h in range(2):
        lse, block = total_map(lambda k, r: rcv_s[k, h, r, :], 8)
        own_s[:, pl.ds(h * BLK, BLK)] = block
        lses.append(lse)
    pot_s[dme] = jnp.concatenate(lses + [jnp.zeros((6, BLK), F32)], axis=0)
    half_at = core * SIDE * BLK

    def cols_of(d2):
        return pl.ds(pl.multiple_of(half_at + d2 * 2 * BLK, 2 * BLK), 2 * BLK)

    def pass_on(d2):
        cols = smap_out.at[:, cols_of(d2)]
        send(cols, cols, sem_swap.at[6], sem_swap.at[7], partner)

    at = pl.ds(pl.multiple_of(half_at + dme * 2 * BLK, 2 * BLK), 2 * BLK)
    smap_out[:, at] = own_s[...]
    for _, dev, _ in d_peers:
        send(pot_s.at[dme], pot_s.at[dme], sem_map.at[6], sem_map.at[7], dev)
        send(own_s, smap_out.at[:, at], sem_map.at[8], sem_ag.at[dme], dev)

    pass_on(dme)
    wait_for(flag_e.at[pl.ds(0, 15)], sem_e.at[1, ITERS])
    over = flag_e[0]
    for k in range(1, 16):
        over = jnp.maximum(over, flag_e[k])
    flag_d[dme] = over
    for _, dev, _ in d_peers:
        send(flag_d.at[dme], flag_d.at[dme], sem_d.at[0, ITERS], sem_d.at[1, ITERS], dev)

    cell_norm = jnp.zeros((8, BLK), F32)
    rows8 = lax.broadcasted_iota(jnp.int32, (8, BLK), 0)
    for b in range(8):
        wide = swap_out[b]
        cell_norm = jnp.where(
            rows8 == b, jnp.sum(wide * wide, axis=0, keepdims=True) * NORM, cell_norm
        )
    cell_own = jnp.where(first, cell_pot[0:8], cell_pot[8:16])
    cpot_out[...] = (cell_own + cell_norm) * (1.0 / UNIT)

    wait_for(pot_s.at[pl.ds(0, 7)], sem_map.at[7])
    lse = jnp.concatenate([pot_s[k, 0:2, :] for k in range(8)], axis=0)
    half_rows = pl.ds(pl.multiple_of(core * SIDE, SIDE), SIDE)
    spot_out[half_rows, :] = (spot_log - lse + spot_norm) * (1.0 / UNIT)
    send(spot_out.at[half_rows], spot_out.at[half_rows], sem_swap.at[4], sem_swap.at[5], partner)
    for _, _, d2 in reversed(d_peers):
        wait_for(own_s, sem_ag.at[d2])
        pass_on(d2)

    wait_for(flag_d.at[pl.ds(0, 7)], sem_d.at[1, ITERS])
    over = flag_d[0]
    for k in range(1, 8):
        over = jnp.maximum(over, flag_d[k])
    flag_out[0] = jnp.max(over).astype(jnp.int32)

    wait_for(cmap_out.at[:, pl.ds(0, 7 * BLK)], sem_map.at[5])
    wait_for(spot_out.at[pl.ds(0, SIDE)], sem_swap.at[5])
    wait_for(smap_out.at[:, pl.ds(0, SIDE * BLK)], sem_swap.at[7])
    wait_for(side_out, sem_swap.at[0])
    wait_for(swap_out, sem_swap.at[2])
    wait_for(spot_out.at[pl.ds(0, SIDE)], sem_swap.at[4])
    wait_for(smap_out.at[:, pl.ds(0, SIDE * BLK)], sem_swap.at[6])
    wait_for(rcv_c.at[pl.ds(0, 15)], sem_map.at[0])
    wait_for(rcv_s.at[pl.ds(0, 7)], sem_map.at[2])
    wait_for(cmap_out.at[:, pl.ds(0, 7 * BLK)], sem_map.at[4])
    wait_for(pot_s.at[pl.ds(0, 7)], sem_map.at[6])
    wait_for(smap_out.at[:, pl.ds(0, 7 * 2 * BLK)], sem_map.at[8])
    wait_for(flag_e.at[pl.ds(0, 15)], sem_e.at[0, ITERS])
    wait_for(flag_d.at[pl.ds(0, 7)], sem_d.at[0, ITERS])

    def sent(it, _):
        wait_for(buf_e.at[it, pl.ds(0, 15)], sem_e.at[0, it])
        wait_for(buf_d.at[it, pl.ds(0, 7)], sem_d.at[0, it])
        return 0

    if quick:
        wait_for(buf_0.at[pl.ds(0, 15)], sem_e.at[0, 0])
        wait_for(buf_d.at[0, pl.ds(0, 7)], sem_d.at[0, 0])
    lax.fori_loop(1 if quick else 0, ITERS - 1, sent, 0)
    wait_for(buf_e.at[ITERS - 1, pl.ds(0, 15)], sem_e.at[0, ITERS - 1])


def run(cap, quick, collective, cfeat, sfeat, cmass, smass, pattern):
    width = 128 if cap <= 128 else 256
    spots = 2 * SIDE if quick else SIDE
    vmem = lambda *shape: pltpu.VMEM(shape, F32)
    half = lambda *shape: pltpu.VMEM(shape, BF16)
    shape = lambda *dims: jax.ShapeDtypeStruct(dims, F32)
    scratch = [
        half(FEAT, 1024), half(FEAT, 4096), vmem(8, BLK), vmem(32, BLK), pltpu.VMEM((8, 32), jnp.int32),
        vmem(8, FEAT, BLK), vmem(8, FEAT, BLK), vmem(2, 8, BLK), vmem(2, 8, BLK),
        half(SIDE, FEAT, BLK), half(SIDE, BLK, FEAT), half(spots, FEAT, BLK), half(spots, BLK, DEEP if quick else FEAT),
        vmem(cap, BLK, BLK), vmem(cap, BLK, BLK), vmem(SIDE, BLK, BLK),
        vmem(cap + 1, FEAT, BLK), vmem(cap + 1, 1, BLK), vmem(2, SIDE, BLK),
        pltpu.VMEM((8, width), jnp.int32), pltpu.SMEM((8, width), jnp.int32),
        pltpu.VMEM((SIDE, BLK), jnp.int32), pltpu.SMEM((SIDE, BLK), jnp.int32),
        vmem(ITERS, 16, SIDE, BLK), vmem(ITERS - 1, 8, SIDE, BLK), vmem(16, 8, BLK), vmem(8, 8, BLK),
        vmem(SIDE, MSG, BLK), vmem(16, MSG, BLK), vmem(SIDE, MSG, BLK), vmem(8, 2, MSG, BLK),
        vmem(FEAT, BLK), vmem(FEAT, 2 * BLK), vmem(8, 8, BLK),
        pltpu.SemaphoreType.DMA((8,)), pltpu.SemaphoreType.DMA((2, ITERS + 1)),
        pltpu.SemaphoreType.DMA((2, ITERS + 1)), pltpu.SemaphoreType.DMA((10,)),
        pltpu.SemaphoreType.DMA((3,)), pltpu.SemaphoreType.DMA((5,)), pltpu.SemaphoreType.DMA((8,)),
    ]
    if quick:
        scratch += [
            vmem(cap, BLK, BLK), vmem(cap, BLK, BLK), vmem(SIDE, BLK), vmem(SIDE, BLK), vmem(SIDE, BLK),
            half(8, DEEP, BLK), pltpu.VMEM((8, BLK), jnp.int32), pltpu.SMEM((8, BLK), jnp.int32),
            vmem(16, 8, BLK),
        ]
    return pl.pallas_call(
        functools.partial(sinkhorn_kernel, cap, quick),
        out_shape=(shape(8, BLK), shape(32, BLK), shape(FEAT, 1024), shape(FEAT, 4096), jax.ShapeDtypeStruct((1,), jnp.int32)),
        in_specs=[pl.BlockSpec(memory_space=pltpu.HBM)] * 5,
        out_specs=tuple([pl.BlockSpec(memory_space=pltpu.VMEM)] * 4 + [pl.BlockSpec(memory_space=pltpu.SMEM)]),
        scratch_shapes=scratch,
        compiler_params=pltpu.CompilerParams(
            collective_id=collective, has_side_effects=True, vmem_limit_bytes=60 * 2**20
        ),
    )(cfeat, sfeat, cmass, smass, pattern)


def place_kernel(*refs):
    srcs, dsts, sems = refs[:4], refs[4:8], refs[8]
    copies = [pltpu.make_async_copy(s, d, sems.at[k]) for k, (s, d) in enumerate(zip(srcs, dsts))]
    for copy in copies:
        copy.start()
    for copy in copies:
        copy.wait()


def place(*arrays):
    return pl.pallas_call(
        place_kernel,
        out_shape=tuple(jax.ShapeDtypeStruct(a.shape, a.dtype) for a in arrays),
        in_specs=[pl.BlockSpec(memory_space=pl.ANY)] * 4,
        out_specs=tuple([pl.BlockSpec(memory_space=pl.ANY)] * 4),
        scratch_shapes=[pltpu.SemaphoreType.DMA((4,))],
    )(*arrays)


def per_device(cell_feat, spot_feat, cell_mass, spot_mass, block_pattern):
    args = (cell_feat.T, spot_feat.T, cell_mass.reshape(8, BLK), spot_mass.reshape(32, BLK), block_pattern)
    outs = run(52, True, 0, *args)
    cpot, spot, cmap, smap = lax.cond(
        outs[4][0] > 0, lambda now: place(*run(SIDE * SIDE, False, 1, *args)[:4]), lambda now: place(*now[:4]), outs
    )
    return cpot.reshape(1024), spot.reshape(4096), cmap.T, smap.T


def solution(mesh):
    in_specs = (P("cells", None), P("spots", None), P("cells"), P("spots"), P("cells", "spots"))
    out_specs = (P("cells"), P("spots"), P("cells", None), P("spots", None))
    return jax.shard_map(
        per_device, mesh=mesh, in_specs=in_specs, out_specs=out_specs, check_vma=False
    )
```

```python
import functools
import math

import jax
import jax.numpy as jnp
from jax import lax
from jax.experimental import pallas as pl
from jax.experimental.pallas import tpu as pltpu
from jax.sharding import PartitionSpec as P

FEAT = 64
BLK = 128
ITERS = 5
EPSILON = 0.05
NEG = -1e30
LOG2E = math.log2(math.e)
UNIT = LOG2E / EPSILON
CROSS = UNIT * 2.0 / FEAT
NORM = UNIT / FEAT
SIDE = 16
FIRST = 56
GAP = 90.0
DEEP = FEAT + 16
MSG = FEAT + 8
MESH = pl.DeviceIdType.MESH
F32 = jnp.float32
BF16 = jnp.bfloat16


def log2(v):
    return jnp.log(v) * LOG2E


def wait_for(view, sem):
    pltpu.make_async_copy(view, view, sem).wait()


def send(src, dst, ssem, rsem, dev):
    pltpu.make_async_remote_copy(
        src_ref=src, dst_ref=dst, send_sem=ssem, recv_sem=rsem, device_id=dev, device_id_type=MESH
    ).start()


def within(index, top):
    return jnp.minimum(jnp.maximum(index, 0), top)


def ring(offset):
    return {0: 0, 1: 1, 2: 2, 3: 1}[offset]


def lane_spread(pot, out):
    for b in range(SIDE):
        out[b] = jnp.transpose(jnp.broadcast_to(pot[b : b + 1], (BLK, BLK)))


def block_list(allowed, lane0, cols, width):
    rows = allowed.shape[0]
    upto = (
        lax.broadcasted_iota(jnp.int32, (BLK, BLK), 0)
        < lax.broadcasted_iota(jnp.int32, (BLK, BLK), 1)
    ).astype(BF16)
    inside = jnp.dot(allowed.astype(BF16), upto, preferred_element_type=F32)
    per_row = jnp.broadcast_to(jnp.sum(allowed, axis=1, keepdims=True), (rows, BLK))
    below = lax.broadcasted_iota(jnp.int32, (rows, BLK), 0)
    before = jnp.zeros((rows, BLK), F32)
    for r in range(rows - 1):
        before = before + jnp.where(below > r, per_row[r : r + 1], 0.0)
    place = jnp.where(allowed > 0, before + inside, -1.0)
    count = jnp.sum(jnp.sum(allowed, axis=1, keepdims=True), axis=0, keepdims=True)
    pairs = rows * cols
    wide_place = jnp.broadcast_to(place[:, None, :], (rows, cols, BLK)).reshape(pairs, BLK)
    pair = lax.broadcasted_iota(jnp.int32, (pairs, BLK), 0)
    pair_lane = lax.broadcasted_iota(jnp.int32, (pairs, BLK), 1)
    chosen = pair_lane == lane0 + pair % cols
    slot_of = jnp.sum(jnp.where(chosen, wide_place, 0.0), axis=1, keepdims=True)
    hot = slot_of == lax.broadcasted_iota(jnp.int32, (pairs, width), 1).astype(F32)
    kind = lax.broadcasted_iota(jnp.int32, (8, pairs), 0)
    which = lax.broadcasted_iota(jnp.int32, (8, pairs), 1)
    facts = jnp.where(kind == 0, which // cols, jnp.where(kind == 1, which % cols, 1))
    lists = jnp.dot(
        facts.astype(F32).astype(BF16), hot.astype(F32).astype(BF16), preferred_element_type=F32
    )
    none = 99.0 * (1.0 - lists[2:3])
    kind = lax.broadcasted_iota(jnp.int32, (8, width), 0)
    lists = jnp.where(kind >= 2, 0.0, lists) + jnp.where(
        kind == 2, lists[0:1] + none, jnp.where(kind == 3, lists[1:2] + none, 0.0)
    )
    return lists, place, count


def sinkhorn_kernel(
    cap, quick, cfeat_h, sfeat_h, cmass_h, smass_h, pattern_h,
    cpot_out, spot_out, cmap_out, smap_out, flag_out,
    cfeat, sfeat, cmass, smass, pattern, swap_out, swap_in, side_out, side_in, chh, cht, shh, sht, cross, crosst, spread,
    blockmap, slot_peak, peak_scr, list_v, list_s, tab_v, tab_s,
    buf_e, buf_d, flag_e, flag_d, msg_c, rcv_c, msg_s, rcv_s, own_c, own_s, pot_s,
    sem_swap, sem_e, sem_d, sem_map, sem_loc, sem_in, sem_ag, *more,
):
    ci = lax.axis_index("cells")
    si = lax.axis_index("spots")
    core = ci % 2
    dme = ci // 2
    ylo, xx = dme // 4, dme % 4
    yhi, zz = si // 4, si % 4
    eme = si * 2 + core
    partner = (ci + 1 - 2 * core, si)

    e_peers = []
    for a in range(2):
        for b in range(4):
            for k in range(2):
                if a or b or k:
                    s2 = lax.rem(yhi + a, 2) * 4 + lax.rem(zz + b, 4)
                    k2 = lax.rem(core + k, 2)
                    e_peers.append((2 * a + ring(b) + 0.1 * k, (dme * 2 + k2, s2), s2, k2))
    e_peers.sort(key=lambda item: -item[0])
    d_peers = []
    for a in range(2):
        for b in range(4):
            if a or b:
                d2 = lax.rem(ylo + a, 2) * 4 + lax.rem(xx + b, 4)
                d_peers.append((a + ring(b), (d2 * 2 + core, si), d2))
    d_peers.sort(key=lambda item: -item[0])

    if quick:
        weight_c, weight_s, bound_c, bound_s, worst, chx, list0_v, list0_s, buf_0 = more

    barrier = pltpu.get_barrier_semaphore()
    for item in e_peers + d_peers:
        pl.semaphore_signal(barrier, inc=1, device_id=item[1], device_id_type=MESH)

    loads = [
        pltpu.make_async_copy(src, dst, sem_in.at[k])
        for k, (src, dst) in enumerate(
            ((pattern_h, pattern), (cfeat_h, cfeat), (sfeat_h, sfeat), (cmass_h, cmass), (smass_h, smass))
        )
    ]
    for load in loads:
        load.start()
    loads[0].wait()
    pattern_own = (pattern[...] > 0).astype(F32)
    side_out[1] = jnp.concatenate([pattern_own, jnp.zeros((8, BLK - 32), F32)], axis=1)
    if quick:
        lists, _, count_0 = block_list(side_out[1], 0, 2 * SIDE, list0_v.shape[1])
        list0_v[...] = lists.astype(jnp.int32)
        copy_0 = pltpu.make_async_copy(list0_v, list0_s, sem_loc.at[2])
        copy_0.start()
    loads[1].wait()
    below = lax.broadcasted_iota(jnp.int32, (DEEP - FEAT, BLK), 0)

    def cells_turned(b, wide):
        cht[b] = jnp.transpose(wide).astype(BF16)

    def own_cells(i, _):
        for k in range(4):
            b = i * 4 + k
            block = cfeat[:, pl.ds(pl.multiple_of(b * BLK, BLK), BLK)]
            wide = block.astype(F32)
            swap_out[b] = wide
            chh[core * 8 + b] = block
            if quick:
                ones = jnp.where(below < 3, 1.0, 0.0).astype(BF16)
                chx[b] = jnp.concatenate([block, ones], axis=0)
            else:
                cells_turned(core * 8 + b, wide)
        return 0

    lax.fori_loop(0, 2, own_cells, 0)
    loads[2].wait()

    spots = 2 * SIDE if quick else SIDE
    offset = 0 if quick else core * SIDE
    mid = core * SIDE if quick else 0

    def own_spots(i, norms):
        for k in range(4):
            b = i * 4 + k
            block = sfeat[:, pl.ds(pl.multiple_of((offset + b) * BLK, BLK), BLK)]
            wide = block.astype(F32)
            norm = jnp.sum(wide * wide, axis=0, keepdims=True)
            shh[b] = block
            if quick:
                rest = norm * -0.5
                parts = jnp.zeros((DEEP - FEAT, BLK), F32)
                for n in range(3):
                    part = rest.astype(BF16).astype(F32)
                    parts = jnp.where(below == n, part, parts)
                    rest = rest - part
                wide = jnp.concatenate([wide, parts], axis=0)
            sht[b] = jnp.transpose(wide).astype(BF16)
            here = lax.broadcasted_iota(jnp.int32, (SIDE, BLK), 0) == b - mid
            norms = jnp.where(here, norm * NORM, norms)
        return norms

    spot_norm = lax.fori_loop(0, spots // 4, own_spots, jnp.zeros((SIDE, BLK), F32))

    def first_half():
        copy_0.wait()
        rows8 = lax.broadcasted_iota(jnp.int32, (8, BLK), 0)
        step = 14

        def body(i, carry):
            peak, total = carry
            parts = []
            for k in range(step):
                e = i * step + k
                r = within(list0_s[0, e], 7)
                c = within(list0_s[1, e], 2 * SIDE - 1)
                v = jnp.dot(sht[c], chx[r], preferred_element_type=F32) * CROSS
                top = jnp.max(v, axis=0, keepdims=True)
                part = jnp.sum(jnp.exp2(v - top), axis=0, keepdims=True)
                parts.append((list0_s[2, e], top, part))
            for at, top, part in parts:
                new = jnp.where(rows8 == at, jnp.maximum(peak, top), peak)
                total = total * jnp.exp2(peak - new) + jnp.where(
                    rows8 == at, part * jnp.exp2(top - new), 0.0
                )
                peak = new
            return peak, total

        init = (jnp.full((8, BLK), NEG, F32), jnp.zeros((8, BLK), F32))
        peak, total = lax.fori_loop(0, FIRST // step, body, init)
        buf_0[eme] = jnp.where(total > 0, peak + log2(jnp.maximum(total, 1e-30)), NEG)
        return jnp.where(count_0 > FIRST, 1.0, 0.0)

    over_0 = first_half() if quick else None
    pl.semaphore_wait(barrier, len(e_peers) + len(d_peers))
    loads[3].wait()
    loads[4].wait()
    side_out[0] = cmass[...]
    if quick:
        for _, dev, _, _ in e_peers:
            send(buf_0.at[eme], buf_0.at[eme], sem_e.at[0, 0], sem_e.at[1, 0], dev)

    send(side_out, side_in, sem_swap.at[0], sem_swap.at[1], partner)
    send(swap_out, swap_in, sem_swap.at[2], sem_swap.at[3], partner)
    wait_for(side_in, sem_swap.at[1])

    first = core == 0
    mine, theirs = side_out[1], side_in[1]
    lane = lax.broadcasted_iota(jnp.int32, (SIDE, BLK), 1)
    both = jnp.concatenate(
        [jnp.where(first, mine, theirs), jnp.where(first, theirs, mine)], axis=0
    )
    both = jnp.where((lane >= core * SIDE) & (lane < core * SIDE + SIDE), both, 0.0)
    lists, place, count = block_list(both, core * SIDE, SIDE, list_v.shape[1])
    over = jnp.broadcast_to(jnp.where(count > cap, 1.0, 0.0), (8, BLK))
    list_v[...] = lists.astype(jnp.int32)
    tab_v[...] = jnp.where((place < 0) | (place >= cap), float(cap), place).astype(jnp.int32)
    copies = [
        pltpu.make_async_copy(list_v, list_s, sem_loc.at[0]),
        pltpu.make_async_copy(tab_v, tab_s, sem_loc.at[1]),
    ]
    for copy in copies:
        copy.start()

    cell_log = log2(
        jnp.concatenate(
            [
                jnp.where(first, side_out[0], side_in[0]),
                jnp.where(first, side_in[0], side_out[0]),
            ],
            axis=0,
        )
    )
    spot_log = log2(smass[pl.ds(pl.multiple_of(core * SIDE, SIDE), SIDE), :])

    if not quick:
        lane_spread(-spot_norm, spread)
    wait_for(swap_in, sem_swap.at[3])

    def other_cells(i, _):
        for k in range(4):
            b = i * 4 + k
            wide = swap_in[b]
            chh[(1 - core) * 8 + b] = wide.astype(BF16)
            cells_turned((1 - core) * 8 + b, wide)
            if quick:
                cells_turned(core * 8 + b, swap_out[b])
        return 0

    lax.fori_loop(0, 2, other_cells, 0)
    for copy in copies:
        copy.wait()

    step = 26 if quick else 8

    def build(with_cross, with_crosst):
        def some(i, _):
            for k in range(step):
                e = i * step + k
                r = within(list_s[0, e], SIDE - 1)
                c = within(list_s[1, e], SIDE - 1)
                if with_cross:
                    cross[e] = jnp.dot(cht[r], shh[mid + c], preferred_element_type=F32) * CROSS
                if with_crosst:
                    crosst[e] = jnp.dot(sht[mid + c, :, :FEAT], chh[r], preferred_element_type=F32) * CROSS
            return 0

        lax.fori_loop(0, cap // step, some, 0)

    build(True, not quick)

    rows = lax.broadcasted_iota(jnp.int32, (SIDE, BLK), 0)

    def half(scores, other, own, feats):
        def body(i, carry):
            peak, total = carry
            parts = []
            for k in range(step):
                e = i * step + k
                o = within(list_s[other, e], SIDE - 1)
                v = scores[e] + spread[o]
                top = jnp.max(v, axis=0, keepdims=True)
                p = jnp.exp2(v - top)
                parts.append((list_s[own + 2, e], top, jnp.sum(p, axis=0, keepdims=True)))
                if feats is not None:
                    slot_peak[e] = top
                    blockmap[e] = jnp.dot(
                        feats(o), p.astype(BF16), preferred_element_type=F32
                    )
            for at, top, part in parts:
                new = jnp.where(rows == at, jnp.maximum(peak, top), peak)
                total = total * jnp.exp2(peak - new) + jnp.where(
                    rows == at, part * jnp.exp2(top - new), 0.0
                )
                peak = new
            return peak, total

        init = (jnp.full((SIDE, BLK), NEG, F32), jnp.zeros((SIDE, BLK), F32))
        return lax.fori_loop(0, cap // step, body, init)

    def joined(peak, total):
        return jnp.where(total > 0, peak + log2(jnp.maximum(total, 1e-30)), NEG)

    def merge(parts):
        top = parts[0]
        for part in parts[1:]:
            top = jnp.maximum(top, part)
        total = jnp.exp2(parts[0] - top)
        for part in parts[1:]:
            total = total + jnp.exp2(part - top)
        return top, total

    def settled(merged):
        return merged[0] + log2(merged[1])

    def cell_send(it, value):
        buf_e[it, eme] = value
        for _, dev, _, _ in e_peers:
            send(buf_e.at[it, eme], buf_e.at[it, eme], sem_e.at[0, it], sem_e.at[1, it], dev)

    def cell_merge(it):
        wait_for(buf_e.at[it, pl.ds(0, 15)], sem_e.at[1, it])
        return merge([buf_e[it, k] for k in range(16)])

    def spot_send(it, value):
        buf_d[it, dme] = value
        for _, dev, _ in d_peers:
            send(buf_d.at[it, dme], buf_d.at[it, dme], sem_d.at[0, it], sem_d.at[1, it], dev)

    def spot_merge(it):
        wait_for(buf_d.at[it, pl.ds(0, 7)], sem_d.at[1, it])
        return merge([buf_d[it, k] for k in range(8)])

    def peaks(i, carry):
        top_c, top_s = carry
        for k in range(step):
            e = i * step + k
            one = jnp.max(crosst[e], axis=0, keepdims=True)
            two = jnp.max(cross[e], axis=0, keepdims=True)
            top_c = jnp.where(rows == list_s[2, e], jnp.maximum(top_c, one), top_c)
            top_s = jnp.where(rows == list_s[3, e], jnp.maximum(top_s, two), top_s)
        return top_c, top_s

    def weights(i, _):
        for k in range(step):
            e = i * step + k
            r = within(list_s[0, e], SIDE - 1)
            c = within(list_s[1, e], SIDE - 1)
            weight_c[e] = jnp.exp2(crosst[e] - bound_c[pl.ds(r, 1), :])
            weight_s[e] = jnp.exp2(cross[e] - bound_s[pl.ds(c, 1), :])
        return 0

    def largest(pot):
        return jnp.max(jnp.max(pot, axis=0, keepdims=True), axis=1, keepdims=True)

    def quick_half(weight, bound, log_mass, merged, shift, other, own):
        lane_spread(jnp.exp2(log_mass - merged[0] - shift) / merged[1], spread)

        def body(i, total):
            parts = []
            for k in range(step):
                e = i * step + k
                o = within(list_s[other, e], SIDE - 1)
                parts.append(
                    (list_s[own + 2, e], jnp.sum(weight[e] * spread[o], axis=0, keepdims=True))
                )
            for at, part in parts:
                total = total + jnp.where(rows == at, part, 0.0)
            return total

        total = lax.fori_loop(0, cap // step, body, jnp.zeros((SIDE, BLK), F32))
        top = bound[...] + shift
        return top, jnp.where(total > 0, top + log2(jnp.maximum(total, 1e-38)), NEG), total

    def watch(top, lse):
        near = (top - lse <= GAP) & (lse - top <= 1.5 * GAP) | (top < 0.5 * NEG) & (lse > 0.5 * NEG)
        worst[...] = jnp.where(near, worst[...], 1.0)

    def first_steps():
        wait_for(buf_0.at[pl.ds(0, 15)], sem_e.at[1, 0])
        cells = jnp.concatenate(
            [settled(merge([buf_0[2 * k + c] for k in range(8)])) for c in range(2)], axis=0
        )
        cells = cell_log - cells
        lane_spread(cells, spread)
        peak, total = half(cross, 0, 1, None)
        spot_send(0, joined(peak, total))
        build(False, True)
        init = jnp.full((SIDE, BLK), NEG, F32)
        top_c, top_s = lax.fori_loop(0, cap // step, peaks, (init, init))
        bound_c[...] = top_c
        bound_s[...] = top_s
        worst[...] = jnp.zeros((SIDE, BLK), F32)
        lax.fori_loop(0, cap // step, weights, 0)
        spots = spot_merge(0)

        def iteration(it, carry):
            spots, shift_c, shift_s = carry
            top, value, _ = quick_half(weight_c, bound_c, spot_log, spots, shift_s, 1, 0)
            cell_send(it, value)
            cells = cell_merge(it)
            top_s, value, _ = quick_half(weight_s, bound_s, cell_log, cells, shift_c, 0, 1)
            spot_send(it, value)
            lse = settled(cells)
            watch(top, lse)
            shift_c = largest(cell_log - lse)
            spots = spot_merge(it)
            lse = settled(spots)
            watch(top_s, lse)
            return spots, shift_c, largest(spot_log - lse)

        carry = (spots, largest(cells), largest(spot_log - settled(spots)))
        spots, _, shift_s = lax.fori_loop(1, ITERS - 1, iteration, carry)
        return over_0, (spots, shift_s)

    def first_steps_whole():
        def iteration(it, _):
            peak, total = half(crosst, 1, 0, None)
            cell_send(it, joined(peak, total))
            lane_spread(cell_log - settled(cell_merge(it)), spread)
            peak, total = half(cross, 0, 1, None)
            spot_send(it, joined(peak, total))
            lane_spread(spot_log - settled(spot_merge(it)), spread)
            return 0

        lax.fori_loop(0, ITERS - 1, iteration, 0)
        return jnp.zeros((1, BLK), F32), None

    more_over, last = first_steps() if quick else first_steps_whole()
    over = jnp.maximum(over, more_over)

    def gather_maps(peak, total, msg, transposed, order, send_pair, plain):
        peak_scr[0] = peak
        peak_scr[1] = total
        blockmap[cap] = jnp.zeros((FEAT, BLK), F32)
        slot_peak[cap] = jnp.full((1, BLK), NEG, F32)

        def one(b):
            top = peak_scr[0, pl.ds(b, 1), :]
            acc = jnp.zeros((FEAT, BLK), F32)
            for k in range(SIDE):
                e = tab_s[k, core * SIDE + b] if transposed else tab_s[b, core * SIDE + k]
                e = within(e, cap)
                acc = acc + (blockmap[e] if plain else blockmap[e] * jnp.exp2(slot_peak[e] - top))
            msg[b, pl.ds(0, FEAT), :] = acc
            msg[b, pl.ds(FEAT, 8), :] = jnp.concatenate(
                [top, peak_scr[1, pl.ds(b, 1), :], jnp.zeros((6, BLK), F32)], axis=0
            )

        if order is None:
            lax.fori_loop(0, SIDE, lambda b, _: (one(b), 0)[1], 0)
        else:
            for d2 in order:
                lax.fori_loop(0, 2, lambda h, _: (one(2 * d2 + h), 0)[1], 0)
                send_pair(d2)

    def total_map(take, n):
        top = take(0, pl.ds(FEAT, 8))[0:1]
        for k in range(1, n):
            top = jnp.maximum(top, take(k, pl.ds(FEAT, 8))[0:1])
        total = jnp.zeros((1, BLK), F32)
        acc = jnp.zeros((FEAT, BLK), F32)
        for k in range(n):
            stat = take(k, pl.ds(FEAT, 8))
            scale = jnp.exp2(stat[0:1] - top)
            total = total + stat[1:2] * scale
            acc = acc + take(k, pl.ds(0, FEAT)) * scale
        return top + log2(total), acc / total

    def send_flag():
        flag_e[eme] = jnp.maximum(over, jnp.max(worst[...], axis=0, keepdims=True)) if quick else over
        for _, dev, _, _ in e_peers:
            send(flag_e.at[eme], flag_e.at[eme], sem_e.at[0, ITERS], sem_e.at[1, ITERS], dev)

    if quick:
        last_top, value, _ = quick_half(weight_c, bound_c, spot_log, last[0], last[1], 1, 0)
        cell_send(ITERS - 1, value)
        peak = last_top

        def quick_maps(i, total):
            parts = []
            for k in range(step):
                e = i * step + k
                o = within(list_s[1, e], SIDE - 1)
                p = (weight_c[e] * spread[o]).astype(BF16)
                blockmap[e] = jnp.dot(shh[mid + o], p, preferred_element_type=F32)
                parts.append((list_s[2, e], jnp.sum(p.astype(F32), axis=0, keepdims=True)))
            for at, part in parts:
                total = total + jnp.where(rows == at, part, 0.0)
            return total

        total = lax.fori_loop(0, cap // step, quick_maps, jnp.zeros((SIDE, BLK), F32))
    else:
        peak, total = half(crosst, 1, 0, lambda o: shh[mid + o])
        cell_send(ITERS - 1, joined(peak, total))
        send_flag()
    gather_maps(peak, total, msg_c, False, None, None, quick)
    for _, dev, s2, k2 in e_peers:
        send(msg_c.at[k2 * 8 + s2], rcv_c.at[eme], sem_map.at[0], sem_map.at[1], dev)
    rcv_c[eme] = msg_c[core * 8 + si]
    cell_lse = settled(cell_merge(ITERS - 1))
    cell_pot = cell_log - cell_lse
    lane_spread(cell_pot, spread)
    if quick:
        watch(last_top, cell_lse)

    peak, total = half(cross, 0, 1, lambda o: chh[o])
    def send_pair(d2):
        for _, dev, other in d_peers:
            if other is d2:
                send(msg_s.at[pl.ds(d2 * 2, 2)], rcv_s.at[dme], sem_map.at[2], sem_map.at[3], dev)

    gather_maps(peak, total, msg_s, True, [d2 for _, _, d2 in d_peers] + [dme], send_pair, False)
    rcv_s[dme] = msg_s[pl.ds(dme * 2, 2)]
    if quick:
        send_flag()

    wait_for(rcv_c.at[pl.ds(0, 15)], sem_map.at[1])
    _, block = total_map(lambda k, r: rcv_c[k, r, :], 16)
    own_c[...] = block
    at = pl.ds(pl.multiple_of(si * BLK, BLK), BLK)
    cmap_out[:, at] = block
    for a in range(2):
        for b in (2, 1, 3, 0):
            if a or b:
                s2 = lax.rem(yhi + a, 2) * 4 + lax.rem(zz + b, 4)
                send(own_c, cmap_out.at[:, at], sem_map.at[4], sem_map.at[5], (ci, s2))

    wait_for(rcv_s.at[pl.ds(0, 7)], sem_map.at[3])
    lses = []
    for h in range(2):
        lse, block = total_map(lambda k, r: rcv_s[k, h, r, :], 8)
        own_s[:, pl.ds(h * BLK, BLK)] = block
        lses.append(lse)
    pot_s[dme] = jnp.concatenate(lses + [jnp.zeros((6, BLK), F32)], axis=0)
    half_at = core * SIDE * BLK

    def cols_of(d2):
        return pl.ds(pl.multiple_of(half_at + d2 * 2 * BLK, 2 * BLK), 2 * BLK)

    def pass_on(d2):
        cols = smap_out.at[:, cols_of(d2)]
        send(cols, cols, sem_swap.at[6], sem_swap.at[7], partner)

    at = pl.ds(pl.multiple_of(half_at + dme * 2 * BLK, 2 * BLK), 2 * BLK)
    smap_out[:, at] = own_s[...]
    for _, dev, _ in d_peers:
        send(pot_s.at[dme], pot_s.at[dme], sem_map.at[6], sem_map.at[7], dev)
        send(own_s, smap_out.at[:, at], sem_map.at[8], sem_ag.at[dme], dev)

    pass_on(dme)
    wait_for(flag_e.at[pl.ds(0, 15)], sem_e.at[1, ITERS])
    over = flag_e[0]
    for k in range(1, 16):
        over = jnp.maximum(over, flag_e[k])
    flag_d[dme] = over
    for _, dev, _ in d_peers:
        send(flag_d.at[dme], flag_d.at[dme], sem_d.at[0, ITERS], sem_d.at[1, ITERS], dev)

    cell_norm = jnp.zeros((8, BLK), F32)
    rows8 = lax.broadcasted_iota(jnp.int32, (8, BLK), 0)
    for b in range(8):
        wide = swap_out[b]
        cell_norm = jnp.where(
            rows8 == b, jnp.sum(wide * wide, axis=0, keepdims=True) * NORM, cell_norm
        )
    cell_own = jnp.where(first, cell_pot[0:8], cell_pot[8:16])
    cpot_out[...] = (cell_own + cell_norm) * (1.0 / UNIT)

    wait_for(pot_s.at[pl.ds(0, 7)], sem_map.at[7])
    lse = jnp.concatenate([pot_s[k, 0:2, :] for k in range(8)], axis=0)
    half_rows = pl.ds(pl.multiple_of(core * SIDE, SIDE), SIDE)
    spot_out[half_rows, :] = (spot_log - lse + spot_norm) * (1.0 / UNIT)
    send(spot_out.at[half_rows], spot_out.at[half_rows], sem_swap.at[4], sem_swap.at[5], partner)
    for _, _, d2 in reversed(d_peers):
        wait_for(own_s, sem_ag.at[d2])
        pass_on(d2)

    wait_for(flag_d.at[pl.ds(0, 7)], sem_d.at[1, ITERS])
    over = flag_d[0]
    for k in range(1, 8):
        over = jnp.maximum(over, flag_d[k])
    flag_out[0] = jnp.max(over).astype(jnp.int32)

    wait_for(cmap_out.at[:, pl.ds(0, 7 * BLK)], sem_map.at[5])
    wait_for(spot_out.at[pl.ds(0, SIDE)], sem_swap.at[5])
    wait_for(smap_out.at[:, pl.ds(0, SIDE * BLK)], sem_swap.at[7])
    wait_for(side_out, sem_swap.at[0])
    wait_for(swap_out, sem_swap.at[2])
    wait_for(spot_out.at[pl.ds(0, SIDE)], sem_swap.at[4])
    wait_for(smap_out.at[:, pl.ds(0, SIDE * BLK)], sem_swap.at[6])
    wait_for(rcv_c.at[pl.ds(0, 15)], sem_map.at[0])
    wait_for(rcv_s.at[pl.ds(0, 7)], sem_map.at[2])
    wait_for(cmap_out.at[:, pl.ds(0, 7 * BLK)], sem_map.at[4])
    wait_for(pot_s.at[pl.ds(0, 7)], sem_map.at[6])
    wait_for(smap_out.at[:, pl.ds(0, 7 * 2 * BLK)], sem_map.at[8])
    wait_for(flag_e.at[pl.ds(0, 15)], sem_e.at[0, ITERS])
    wait_for(flag_d.at[pl.ds(0, 7)], sem_d.at[0, ITERS])

    def sent(it, _):
        wait_for(buf_e.at[it, pl.ds(0, 15)], sem_e.at[0, it])
        wait_for(buf_d.at[it, pl.ds(0, 7)], sem_d.at[0, it])
        return 0

    if quick:
        wait_for(buf_0.at[pl.ds(0, 15)], sem_e.at[0, 0])
        wait_for(buf_d.at[0, pl.ds(0, 7)], sem_d.at[0, 0])
    lax.fori_loop(1 if quick else 0, ITERS - 1, sent, 0)
    wait_for(buf_e.at[ITERS - 1, pl.ds(0, 15)], sem_e.at[0, ITERS - 1])


def run(cap, quick, collective, cfeat, sfeat, cmass, smass, pattern):
    width = 128 if cap <= 128 else 256
    spots = 2 * SIDE if quick else SIDE
    vmem = lambda *shape: pltpu.VMEM(shape, F32)
    half = lambda *shape: pltpu.VMEM(shape, BF16)
    shape = lambda *dims: jax.ShapeDtypeStruct(dims, F32)
    scratch = [
        half(FEAT, 1024), half(FEAT, 4096), vmem(8, BLK), vmem(32, BLK), pltpu.VMEM((8, 32), jnp.int32),
        vmem(8, FEAT, BLK), vmem(8, FEAT, BLK), vmem(2, 8, BLK), vmem(2, 8, BLK),
        half(SIDE, FEAT, BLK), half(SIDE, BLK, FEAT), half(spots, FEAT, BLK), half(spots, BLK, DEEP if quick else FEAT),
        vmem(cap, BLK, BLK), vmem(cap, BLK, BLK), vmem(SIDE, BLK, BLK),
        vmem(cap + 1, FEAT, BLK), vmem(cap + 1, 1, BLK), vmem(2, SIDE, BLK),
        pltpu.VMEM((8, width), jnp.int32), pltpu.SMEM((8, width), jnp.int32),
        pltpu.VMEM((SIDE, BLK), jnp.int32), pltpu.SMEM((SIDE, BLK), jnp.int32),
        vmem(ITERS, 16, SIDE, BLK), vmem(ITERS - 1, 8, SIDE, BLK), vmem(16, 8, BLK), vmem(8, 8, BLK),
        vmem(SIDE, MSG, BLK), vmem(16, MSG, BLK), vmem(SIDE, MSG, BLK), vmem(8, 2, MSG, BLK),
        vmem(FEAT, BLK), vmem(FEAT, 2 * BLK), vmem(8, 8, BLK),
        pltpu.SemaphoreType.DMA((8,)), pltpu.SemaphoreType.DMA((2, ITERS + 1)),
        pltpu.SemaphoreType.DMA((2, ITERS + 1)), pltpu.SemaphoreType.DMA((10,)),
        pltpu.SemaphoreType.DMA((3,)), pltpu.SemaphoreType.DMA((5,)), pltpu.SemaphoreType.DMA((8,)),
    ]
    if quick:
        scratch += [
            vmem(cap, BLK, BLK), vmem(cap, BLK, BLK), vmem(SIDE, BLK), vmem(SIDE, BLK), vmem(SIDE, BLK),
            half(8, DEEP, BLK), pltpu.VMEM((8, BLK), jnp.int32), pltpu.SMEM((8, BLK), jnp.int32),
            vmem(16, 8, BLK),
        ]
    return pl.pallas_call(
        functools.partial(sinkhorn_kernel, cap, quick),
        out_shape=(shape(8, BLK), shape(32, BLK), shape(FEAT, 1024), shape(FEAT, 4096), jax.ShapeDtypeStruct((1,), jnp.int32)),
        in_specs=[pl.BlockSpec(memory_space=pltpu.HBM)] * 5,
        out_specs=tuple([pl.BlockSpec(memory_space=pltpu.VMEM)] * 4 + [pl.BlockSpec(memory_space=pltpu.SMEM)]),
        scratch_shapes=scratch,
        compiler_params=pltpu.CompilerParams(
            collective_id=collective, has_side_effects=True, vmem_limit_bytes=60 * 2**20
        ),
    )(cfeat, sfeat, cmass, smass, pattern)


def place_kernel(*refs):
    srcs, dsts, sems = refs[:4], refs[4:8], refs[8]
    copies = [pltpu.make_async_copy(s, d, sems.at[k]) for k, (s, d) in enumerate(zip(srcs, dsts))]
    for copy in copies:
        copy.start()
    for copy in copies:
        copy.wait()


def place(*arrays):
    return pl.pallas_call(
        place_kernel,
        out_shape=tuple(jax.ShapeDtypeStruct(a.shape, a.dtype) for a in arrays),
        in_specs=[pl.BlockSpec(memory_space=pl.ANY)] * 4,
        out_specs=tuple([pl.BlockSpec(memory_space=pl.ANY)] * 4),
        scratch_shapes=[pltpu.SemaphoreType.DMA((4,))],
    )(*arrays)


def per_device(cell_feat, spot_feat, cell_mass, spot_mass, block_pattern):
    args = (cell_feat.T, spot_feat.T, cell_mass.reshape(8, BLK), spot_mass.reshape(32, BLK), block_pattern)
    outs = run(52, True, 0, *args)
    cpot, spot, cmap, smap = lax.cond(
        outs[4][0] > 0, lambda now: place(*run(SIDE * SIDE, False, 1, *args)[:4]), lambda now: place(*now[:4]), outs
    )
    return cpot.reshape(1024), spot.reshape(4096), cmap.T, smap.T


def solution(mesh):
    in_specs = (P("cells", None), P("spots", None), P("cells"), P("spots"), P("cells", "spots"))
    out_specs = (P("cells"), P("spots"), P("cells", None), P("spots", None))
    return jax.shard_map(
        per_device, mesh=mesh, in_specs=in_specs, out_specs=out_specs, check_vma=False
    )
```
